128 devices in a mesh: occ: 4 (over z_lo, core), aux: 32 (over y, z_hi, x).
Axes of the slice: x: 4, y: 4, z: 4 (z_hi: 2, z_lo: 2; z = z_hi * 2 + z_lo), core: 2. Of those that a mesh axis runs over, the one named last changes fastest.
Arguments:
- three_index: bfloat16 [768, 32, 20480], P(None, 'occ', 'aux'), may hold values from -6 to 6
- tile_mask: int32 [4, 6], replicated, may hold values from 0 to 1, as said below
- occ_density: bfloat16 [32, 32], replicated, may hold values from -1 to 1
- virt_density: bfloat16 [768, 768], replicated, may hold values from -0.21875 to 0.21875
Outputs:
- gamma: bfloat16 [768, 32, 20480], P('aux', 'occ')
The draws below stay inside these ranges and needn't reach their ends.
Inputs may be any that keep to these rules, and one draw needn't show every extreme that they name: `tile_mask`: each slab's row holds between 2 and 4 ones, and some slab's row holds exactly 4.
All inputs are finite; a program needn't handle non-finite values.
Results may differ from the reference program's by a relative error of at most 0.001.
Values may be sent and summed in bfloat16 or wider, within the bound.
No kernel may reach another device: no remote copies, remote signals or barrier semaphores. Data moves between devices by JAX's collectives and lax.ppermute only.
A program may use at most 256 MiB of HBM per device.

```python
import jax
import jax.numpy as jnp
from jax import lax

OCC_DEV = 8
VT = 6
VTILE = 128
CAP = 4
NAUX = 20480
NV = 768
NOCC = 32
NSLAB = 4
N_AUX = 32


def draw_tile_mask(key, part):
    key = jax.random.fold_in(key, 11)
    first, second, third = jax.random.split(key, 3)
    counts = jax.random.randint(first, (NSLAB,), 2, CAP + 1)
    fullest = jax.random.randint(second, (), 0, NSLAB)
    counts = jnp.where(jnp.arange(NSLAB) == fullest, CAP, counts)
    ranking = jax.vmap(lambda row_key: jax.random.permutation(row_key, VT))(jax.random.split(third, NSLAB))
    return (ranking < counts[:, None]).astype(jnp.int32)


def levels(stream_key, shape, cuts, low, largest):
    gain = 1.0
    for position, blocks in cuts:
        heights = jax.random.uniform(jax.random.fold_in(jax.random.fold_in(stream_key, 6), position), (blocks,), jnp.float32, low / len(cuts), largest / len(cuts))
        gain = gain * jnp.repeat(jnp.exp(heights), shape[position] // blocks).reshape((-1,) + (1,) * (len(shape) - 1 - position))
    return gain


def noise(key, shape, scale, most, shards=(), kind=jnp.bfloat16):
    gain = levels(key, shape, shards, -0.22, 0.18) if shards else 1.0
    entries = jax.random.normal(key, shape, jnp.float32) * scale * gain
    return jnp.minimum(jnp.maximum(entries, -most), most).astype(kind)


def setup_inputs(seed: int = 0) -> dict:
    keys = jax.random.split(jax.random.key(seed), 5)
    three_index = noise(keys[0], (NV, NOCC, NAUX), 1.0, 6.0, ((1, 4), (2, 32)))
    tile_mask = draw_tile_mask(jax.random.fold_in(keys[4], 71), 0)
    occ_density = noise(keys[2], (NOCC, NOCC), NOCC ** -0.5, 1.0)
    virt_density = noise(keys[3], (NV, NV), NV ** -0.5, 0.21875)
    return dict(three_index=three_index, tile_mask=tile_mask, occ_density=occ_density, virt_density=virt_density)


def masked_input(three_index, tile_mask):
    virt_tile = jnp.arange(NV, dtype=jnp.int32) // VTILE
    occ_slab = jnp.arange(NOCC, dtype=jnp.int32) // OCC_DEV
    keep_mask = tile_mask[occ_slab][:, virt_tile]
    return three_index * jnp.transpose(keep_mask).astype(jnp.bfloat16)[:, :, None]


def reference(three_index, tile_mask, occ_density, virt_density):
    masked = masked_input(three_index, tile_mask)
    aux_width = NAUX // N_AUX
    blocks = jnp.transpose(masked.reshape(NV, NOCC, N_AUX, aux_width), (2, 0, 1, 3))
    occ_full = occ_density.astype(jnp.float32)

    def one_block(aux_block):
        occupied = jnp.einsum("ij,ajp->aip", occ_full, aux_block.astype(jnp.float32))
        virtual = jnp.dot(virt_density, aux_block.reshape(NV, NOCC * aux_width), preferred_element_type=jnp.float32)
        return (occupied + virtual.reshape(NV, NOCC, aux_width)).astype(jnp.bfloat16)

    result = lax.map(one_block, blocks)
    return jnp.transpose(result, (1, 2, 0, 3)).reshape(NV, NOCC, NAUX)
```

```python
import jax
import jax.numpy as jnp
from jax import lax
from jax.experimental import pallas as pl
from jax.experimental.pallas import tpu as pltpu
from jax.sharding import PartitionSpec as P

VT = 6
CAP = 4
OCC = 8
SLABS = 4
FLIPS = (0, 2, 1, 3)
LANES = 128
GROUP = 32
ROWS = GROUP * OCC
FINE = 16
FROWS = FINE * OCC
HALVES = 2
INNER = 4
VMEM = 60 << 20


def iota(shape, dim):
    return lax.broadcasted_iota(jnp.int32, shape, dim)


def one_hot(condition):
    return jnp.where(condition, 1.0, 0.0).astype(jnp.bfloat16)


def dot(left, right):
    return jnp.dot(left, right, preferred_element_type=jnp.float32)


def permutation(back):
    shape = (ROWS, ROWS)
    fine, coarse = (iota(shape, 1), iota(shape, 0)) if back else (iota(shape, 0), iota(shape, 1))
    return one_hot((fine % GROUP == coarse // OCC) & (fine // GROUP == coarse % OCC))


def tile_of(mask_ref, slab, q):
    seen, tile = 0, 0
    for t in range(VT):
        seen = seen + mask_ref[slab, t]
        tile = tile + (seen <= q).astype(jnp.int32)
    return jnp.minimum(tile, VT - 1)


def transpose_rows(perm, columns):
    y = dot(perm, jnp.concatenate(columns, axis=1)).astype(jnp.bfloat16)
    return y[:, :LANES], y[:, LANES:]


def pack_rows(perm, x_ref, outs, first):
    for g in range(0, x_ref.shape[0] // GROUP, 2):
        for c, out in enumerate(outs):
            cols = slice((first + c) * LANES, (first + c + 1) * LANES)
            pair = transpose_rows(perm, [
                x_ref[n * GROUP:(n + 1) * GROUP, :, cols].reshape(ROWS, LANES) for n in (g, g + 1)
            ])
            for n in range(2):
                at = (g + n) * GROUP
                out[:, at:at + GROUP, :] = pair[n].reshape(OCC, GROUP, LANES)


def first_body(mask_ref, ids_ref, x_ref, out):
    pack_rows(permutation(False), x_ref, [out], 0)


def first_pack(mask, ids, three_index):
    tile = three_index.shape[0] // VT
    return pl.pallas_call(
        first_body,
        out_shape=jax.ShapeDtypeStruct((OCC, CAP * tile, LANES), jnp.bfloat16),
        grid_spec=pltpu.PrefetchScalarGridSpec(
            num_scalar_prefetch=2,
            grid=(CAP,),
            in_specs=[
                pl.BlockSpec((tile, OCC, LANES), lambda q, mask, ids: (tile_of(mask, ids[0], q), 0, 0)),
            ],
            out_specs=pl.BlockSpec((OCC, tile, LANES), lambda q, mask, ids: (0, q, 0)),
        ),
        compiler_params=pltpu.CompilerParams(vmem_limit_bytes=VMEM),
        cost_estimate=pl.CostEstimate(flops=1 << 29, bytes_accessed=2 << 20, transcendentals=0),
    )(mask, ids, three_index)


def rest_body(mask_ref, ids_ref, x_ref, v0_ref, v1_ref, d_ref, virt_out, occ_out, table_out, *outs):
    q = pl.program_id(0)
    own = ids_ref[0]
    pack_rows(permutation(False), x_ref, outs, 1)
    for which, v_ref in enumerate((v0_ref, v1_ref)):
        count = 0
        for t in range(VT):
            count = count + mask_ref[own ^ FLIPS[which], t]
        part = v_ref[...].reshape(-1, x_ref.shape[0])
        virt_out[which] = jnp.where(q < count, part, jnp.zeros_like(part))

    @pl.when(q == 0)
    def _():
        tile = x_ref.shape[0]
        for s in range(SLABS):
            seen = 0
            for t in range(VT):
                here = mask_ref[own ^ FLIPS[s], t]
                table_out[s, t] = jnp.where(here > 0, seen * tile, -1)
                seen = seen + here
        width = SLABS * FROWS
        shape = (SLABS * OCC, width)
        col = iota(shape, 1)
        slab = col // FROWS
        source = own
        for s in range(1, SLABS):
            source = jnp.where(slab == s, own ^ FLIPS[s], source)
        pick_cols = one_hot(iota(shape, 0) == source * OCC + col % FROWS // FINE)
        spread = dot(d_ref[...], pick_cols).astype(jnp.bfloat16)
        shape = (FROWS, SLABS * OCC)
        full = (FROWS, width)
        same = iota(full, 0) % FINE == iota(full, 1) % FINE
        for which in range(2):
            pick_rows = one_hot(iota(shape, 1) == (own ^ FLIPS[which]) * OCC + iota(shape, 0) // FINE)
            occ_out[which] = jnp.where(same, dot(pick_rows, spread), 0.0).astype(jnp.bfloat16)


def rest_pack(mask, ids, three_index, by_half, occ_density):
    virt_count, _, cols = three_index.shape
    tile = virt_count // VT
    blocks, _, span, _ = by_half.shape
    half_rows = blocks * span
    count = cols // LANES - 1

    def half_block(which):
        def index(q, mask, ids):
            half = ids[1] if which == 0 else 1 - ids[1]
            return 0, half, 0, tile_of(mask, ids[0] ^ FLIPS[which], q)
        return pl.BlockSpec((blocks, 1, span, tile), index)

    virt, occ, table, *packs = pl.pallas_call(
        rest_body,
        out_shape=[
            jax.ShapeDtypeStruct((2, half_rows, CAP * tile), jnp.bfloat16),
            jax.ShapeDtypeStruct((2, FROWS, SLABS * FROWS), jnp.bfloat16),
            jax.ShapeDtypeStruct((SLABS, VT), jnp.int32),
        ] + [jax.ShapeDtypeStruct((OCC, CAP * tile, LANES), jnp.bfloat16)] * count,
        grid_spec=pltpu.PrefetchScalarGridSpec(
            num_scalar_prefetch=2,
            grid=(CAP,),
            in_specs=[
                pl.BlockSpec((tile, OCC, cols), lambda q, mask, ids: (tile_of(mask, ids[0], q), 0, 0)),
                half_block(0),
                half_block(1),
                pl.BlockSpec(occ_density.shape, lambda q, mask, ids: (0, 0)),
            ],
            out_specs=[
                pl.BlockSpec((2, half_rows, tile), lambda q, mask, ids: (0, 0, q)),
                pl.BlockSpec((2, FROWS, SLABS * FROWS), lambda q, mask, ids: (0, 0, 0)),
                pl.BlockSpec(memory_space=pltpu.SMEM),
            ] + [pl.BlockSpec((OCC, tile, LANES), lambda q, mask, ids: (0, q, 0))] * count,
        ),
        compiler_params=pltpu.CompilerParams(vmem_limit_bytes=VMEM),
        cost_estimate=pl.CostEstimate(flops=3 << 30, bytes_accessed=12 << 20, transcendentals=0),
    )(mask, ids, three_index, by_half, by_half, occ_density)
    return packs, virt, occ, table


def density_body(table_ref, ids_ref, x0, x1, x2, x3, virt_in, occ_in, out, packs, virt_ref, occ_ref, total, mixed, result, in_sems, out_sems):
    depth = x0.shape[1]
    half_rows = virt_ref.shape[1]
    blocks = out.shape[0] // (INNER * HALVES * OCC * 24)
    span = half_rows // blocks
    tile = depth // CAP
    targets = [packs.at[s, :, pl.ds(0, depth), :] for s in range(SLABS)] + [virt_ref, occ_ref]
    arrivals = [
        pltpu.make_async_copy(ref, target, in_sems.at[n])
        for n, (ref, target) in enumerate(zip((x0, x1, x2, x3, virt_in, occ_in), targets))
    ]
    for n in (0, 4, 1, 2, 3, 5):
        arrivals[n].start()
    for s in range(SLABS):
        packs[s, :, depth:depth + FINE, :] = jnp.zeros((OCC, FINE, LANES), jnp.bfloat16)
    perm = permutation(True)
    arrivals[4].wait()
    for which in range(2):
        arrivals[which].wait()
        for i in range(0, OCC, 2):
            both = jnp.concatenate([packs[which, i, :depth], packs[which, i + 1, :depth]], axis=1)
            y = dot(virt_ref[which], both)
            total[which, i] = y[:, :LANES]
            total[which, i + 1] = y[:, LANES:]
    for n in (2, 3, 5):
        arrivals[n].wait()
    departures = []
    for which in range(2):
        half = ids_ref[1] if which == 0 else 1 - ids_ref[1]
        for first in range(0, half_rows, 2 * FINE):
            columns, added = [], []
            for row in (first, first + FINE):
                start = row // span * (HALVES * span) + row % span + half * span
                parts = []
                for s in range(SLABS):
                    base = table_ref[s, start // tile]
                    at = pl.multiple_of(jnp.where(base < 0, depth, base + start % tile), FINE)
                    parts.append(packs[s, :, pl.ds(at, FINE), :].reshape(FROWS, LANES))
                columns.append(jnp.concatenate(parts, axis=0))
                added.append(total[which, :, row:row + FINE, :].reshape(FROWS, LANES))
            y = dot(occ_ref[which], jnp.concatenate(columns, axis=1))
            y = (y + jnp.concatenate(added, axis=1)).astype(jnp.bfloat16)
            for n in range(2):
                row = first + n * FINE
                mixed[which, :, row:row + FINE, :] = y[:, n * LANES:(n + 1) * LANES].reshape(OCC, FINE, LANES)
        for first in range(0, half_rows, 2 * GROUP):
            pair = transpose_rows(perm, [
                mixed[which, :, row:row + GROUP, :].reshape(ROWS, LANES) for row in (first, first + GROUP)
            ])
            for n in range(2):
                at = (first + n * GROUP) * OCC
                result[which, at:at + ROWS, :] = pair[n]
        for b in range(blocks):
            start = pl.multiple_of((b * HALVES + half) * span * OCC, span * OCC)
            copy = pltpu.make_async_copy(
                result.at[which, pl.ds(b * span * OCC, span * OCC), :],
                out.at[pl.ds(start, span * OCC), :],
                out_sems.at[which * blocks + b],
            )
            copy.start()
            departures.append(copy)
    for copy in departures:
        copy.wait()


def density(table, ids, packs, virt, occ):
    depth = packs[0].shape[1]
    half_rows = virt.shape[1]
    rows = 2 * half_rows * OCC
    blocks = rows // (INNER * HALVES * OCC * 24)
    return pl.pallas_call(
        density_body,
        out_shape=jax.ShapeDtypeStruct((rows, LANES), jnp.bfloat16),
        grid_spec=pltpu.PrefetchScalarGridSpec(
            num_scalar_prefetch=2,
            grid=(1,),
            in_specs=[pl.BlockSpec(memory_space=pl.ANY)] * SLABS + [pl.BlockSpec(memory_space=pltpu.HBM)] * 2,
            out_specs=pl.BlockSpec(memory_space=pl.ANY),
            scratch_shapes=[
                pltpu.VMEM((SLABS, OCC, depth + FINE, LANES), jnp.bfloat16),
                pltpu.VMEM(virt.shape, jnp.bfloat16),
                pltpu.VMEM(occ.shape, jnp.bfloat16),
                pltpu.VMEM((2, OCC, half_rows, LANES), jnp.float32),
                pltpu.VMEM((2, OCC, half_rows, LANES), jnp.bfloat16),
                pltpu.VMEM((2, half_rows * OCC, LANES), jnp.bfloat16),
                pltpu.SemaphoreType.DMA((SLABS + 2,)),
                pltpu.SemaphoreType.DMA((2 * blocks,)),
            ],
        ),
        compiler_params=pltpu.CompilerParams(vmem_limit_bytes=24 << 20),
        cost_estimate=pl.CostEstimate(
            flops=2 * LANES * (rows * depth + 3 * rows * ROWS),
            bytes_accessed=2 * LANES * (rows + SLABS * OCC * depth),
            transcendentals=0,
        ),
    )(table, ids, *packs, virt, occ)


def assemble_body(*refs):
    count = len(refs) - 5
    ins, out = refs[:count], refs[count]
    arrived, whole, in_sems, out_sems = refs[count + 1:]
    rows = out.shape[0]
    peers = ins[0].shape[0] // rows
    cols = out.shape[2] // peers
    step = peers // out_sems.shape[0]
    arrivals = [pltpu.make_async_copy(ref, arrived.at[k], in_sems.at[k]) for k, ref in enumerate(ins)]
    for copy in arrivals:
        copy.start()

    def take(k, m):
        whole[:, :, m * cols + k * LANES:m * cols + (k + 1) * LANES] = arrived[k, m * rows:(m + 1) * rows]

    for k in range(count - 1):
        arrivals[k].wait()
        for m in range(peers):
            take(k, m)
    arrivals[-1].wait()
    departures = []
    for n in range(peers // step):
        for m in range(n * step, (n + 1) * step):
            take(count - 1, m)
        part = pl.ds(n * step * cols, step * cols)
        copy = pltpu.make_async_copy(whole.at[:, :, part], out.at[:, :, part], out_sems.at[n])
        copy.start()
        departures.append(copy)
    for copy in departures:
        copy.wait()


def assemble(parts, peers):
    rows = parts[0].shape[0] // peers
    shape = (rows, OCC, peers * len(parts) * LANES)
    return pl.pallas_call(
        assemble_body,
        out_shape=jax.ShapeDtypeStruct(shape, jnp.bfloat16),
        in_specs=[pl.BlockSpec(memory_space=pl.ANY)] * len(parts),
        out_specs=pl.BlockSpec(memory_space=pl.ANY),
        scratch_shapes=[
            pltpu.VMEM((len(parts),) + parts[0].shape, jnp.bfloat16),
            pltpu.VMEM(shape, jnp.bfloat16),
            pltpu.SemaphoreType.DMA((len(parts),)),
            pltpu.SemaphoreType.DMA((8,)),
        ],
        compiler_params=pltpu.CompilerParams(vmem_limit_bytes=VMEM),
        cost_estimate=pl.CostEstimate(
            flops=0, bytes_accessed=4 * rows * OCC * shape[2], transcendentals=0
        ),
    )(*parts)


def exchange_groups(peers):
    groups = []
    for parity in range(2):
        for core in range(2):
            groups.append([
                (2 * (((k // INNER) % HALVES) ^ parity) + core) * peers + k for k in range(peers)
            ])
    return groups


def local(three_index, tile_mask, occ_density, virt_density):
    virt_count = three_index.shape[0]
    peers = lax.axis_size("aux")
    own = lax.axis_index("occ")
    my_half = (lax.axis_index("aux") // INNER) % HALVES
    ids = jnp.stack([own, my_half]).astype(jnp.int32)
    by_half = virt_density.reshape(peers // (HALVES * INNER), HALVES, -1, virt_count)

    head = first_pack(tile_mask, ids, three_index)
    others, *weights = rest_pack(tile_mask, ids, three_index, by_half, occ_density)
    virt, occ, table = (pltpu.with_memory_space_constraint(array, pltpu.HBM) for array in weights)
    mine = [head] + others

    chip_pairs = [(s, s ^ 2) for s in range(SLABS)]
    core_pairs = [(s, s ^ 1) for s in range(SLABS)]
    groups = exchange_groups(peers)
    done, acrosses = [], []
    for k, part in enumerate(mine):
        sent = part
        if k >= 2:
            sent, _ = lax.optimization_barrier((part, acrosses[k - 2]))
        across = lax.ppermute(sent, "occ", chip_pairs)
        across, _ = lax.optimization_barrier((across, gamma if k else mine[1]))
        acrosses.append(across)
        beside = lax.ppermute(part, "occ", core_pairs)
        diagonal = lax.ppermute(across, "occ", core_pairs)
        gamma = density(table, ids, (part, across, beside, diagonal), virt, occ)
        gamma = gamma.reshape(virt_count, OCC, -1)
        done.append(lax.all_to_all(
            gamma, ("occ", "aux"), split_axis=0, concat_axis=0, axis_index_groups=groups, tiled=True
        ))
    return assemble(done, peers)


def solution(mesh):
    return jax.shard_map(
        local,
        mesh=mesh,
        in_specs=(P(None, "occ", "aux"), P(), P(), P()),
        out_specs=P("aux", "occ", None),
        check_vma=False,
    )
```

```python
import functools

import jax
import jax.numpy as jnp
from jax import lax
from jax.experimental import pallas as pl
from jax.experimental.pallas import tpu as pltpu
from jax.sharding import PartitionSpec as P

VT = 6
CAP = 4
OCC = 8
SLABS = 4
FLIPS = (0, 2, 1, 3)
LANES = 128
GROUP = 32
ROWS = GROUP * OCC
FINE = 16
FROWS = FINE * OCC
HALVES = 2
SPAN = 96
INNER = 4
VMEM = 60 << 20


def iota(shape, dim):
    return lax.broadcasted_iota(jnp.int32, shape, dim)


def one_hot(condition):
    return jnp.where(condition, 1.0, 0.0).astype(jnp.bfloat16)


def dot(left, right):
    return jnp.dot(left, right, preferred_element_type=jnp.float32)


def permutation(back):
    shape = (ROWS, ROWS)
    fine, coarse = (iota(shape, 1), iota(shape, 0)) if back else (iota(shape, 0), iota(shape, 1))
    return one_hot((fine % GROUP == coarse // OCC) & (fine // GROUP == coarse % OCC))


def tile_of(mask_ref, slab, q):
    seen, tile = 0, 0
    for t in range(VT):
        seen = seen + mask_ref[slab, t]
        tile = tile + (seen <= q).astype(jnp.int32)
    return jnp.minimum(tile, VT - 1)


def transpose_rows(perm, columns):
    y = dot(perm, jnp.concatenate(columns, axis=1)).astype(jnp.bfloat16)
    return y[:, :LANES], y[:, LANES:]


def pack_rows(perm, x_ref, outs, first):
    for g in range(0, x_ref.shape[0] // GROUP, 2):
        for c, out in enumerate(outs):
            cols = slice((first + c) * LANES, (first + c + 1) * LANES)
            pair = transpose_rows(perm, [
                x_ref[n * GROUP:(n + 1) * GROUP, :, cols].reshape(ROWS, LANES) for n in (g, g + 1)
            ])
            for n in range(2):
                at = (g + n) * GROUP
                out[:, at:at + GROUP, :] = pair[n].reshape(OCC, GROUP, LANES)


def first_body(mask_ref, x_ref, out, tiles, packed, in_sems, out_sems):
    tile = tiles.shape[1]
    own = lax.axis_index("occ")
    arrivals, departures = [], []
    for q in range(CAP):
        at = pl.multiple_of(tile_of(mask_ref, own, q) * tile, tile)
        copy = pltpu.make_async_copy(x_ref.at[pl.ds(at, tile), :, pl.ds(0, LANES)], tiles.at[q], in_sems.at[q])
        copy.start()
        arrivals.append(copy)
    perm = permutation(False)
    for q in range(CAP):
        arrivals[q].wait()
        pack_rows(perm, tiles.at[q], [packed.at[q]], 0)
        copy = pltpu.make_async_copy(packed.at[q], out.at[:, pl.ds(q * tile, tile), :], out_sems.at[q])
        copy.start()
        departures.append(copy)
    for copy in departures:
        copy.wait()


def first_pack(mask, three_index):
    tile = three_index.shape[0] // VT
    return pl.pallas_call(
        first_body,
        out_shape=jax.ShapeDtypeStruct((OCC, CAP * tile, LANES), jnp.bfloat16),
        grid_spec=pltpu.PrefetchScalarGridSpec(
            num_scalar_prefetch=1,
            grid=(1,),
            in_specs=[pl.BlockSpec(memory_space=pl.ANY)],
            out_specs=pl.BlockSpec(memory_space=pl.ANY),
            scratch_shapes=[
                pltpu.VMEM((CAP, tile, OCC, LANES), jnp.bfloat16),
                pltpu.VMEM((CAP, OCC, tile, LANES), jnp.bfloat16),
                pltpu.SemaphoreType.DMA((CAP,)),
                pltpu.SemaphoreType.DMA((CAP,)),
            ],
        ),
        compiler_params=pltpu.CompilerParams(vmem_limit_bytes=VMEM),
        cost_estimate=pl.CostEstimate(flops=1 << 29, bytes_accessed=2 << 20, transcendentals=0),
    )(mask, three_index)


def rest_body(mask_ref, ids_ref, x_ref, v0_ref, v1_ref, d_ref, virt_out, occ_out, table_out, *outs):
    q = pl.program_id(0)
    own = ids_ref[0]
    pack_rows(permutation(False), x_ref, outs, 1)
    for which, v_ref in enumerate((v0_ref, v1_ref)):
        count = 0
        for t in range(VT):
            count = count + mask_ref[own ^ FLIPS[which], t]
        part = v_ref[...].reshape(-1, x_ref.shape[0])
        virt_out[which] = jnp.where(q < count, part, jnp.zeros_like(part))

    @pl.when(q == 0)
    def _():
        tile = x_ref.shape[0]
        for s in range(SLABS):
            seen = 0
            for t in range(VT):
                here = mask_ref[own ^ FLIPS[s], t]
                table_out[s, t] = jnp.where(here > 0, seen * tile, -1)
                seen = seen + here
        width = SLABS * FROWS
        shape = (SLABS * OCC, width)
        col = iota(shape, 1)
        slab = col // FROWS
        source = own
        for s in range(1, SLABS):
            source = jnp.where(slab == s, own ^ FLIPS[s], source)
        pick_cols = one_hot(iota(shape, 0) == source * OCC + col % FROWS // FINE)
        spread = dot(d_ref[...], pick_cols).astype(jnp.bfloat16)
        shape = (FROWS, SLABS * OCC)
        full = (FROWS, width)
        same = iota(full, 0) % FINE == iota(full, 1) % FINE
        for which in range(2):
            pick_rows = one_hot(iota(shape, 1) == (own ^ FLIPS[which]) * OCC + iota(shape, 0) // FINE)
            occ_out[which] = jnp.where(same, dot(pick_rows, spread), 0.0).astype(jnp.bfloat16)


def rest_pack(mask, ids, three_index, by_half, occ_density):
    virt_count, _, cols = three_index.shape
    tile = virt_count // VT
    blocks, _, span, _ = by_half.shape
    half_rows = blocks * span
    count = cols // LANES - 1

    def half_block(which):
        def index(q, mask, ids):
            half = ids[1] if which == 0 else 1 - ids[1]
            return 0, half, 0, tile_of(mask, ids[0] ^ FLIPS[which], q)
        return pl.BlockSpec((blocks, 1, span, tile), index)

    virt, occ, table, *packs = pl.pallas_call(
        rest_body,
        out_shape=[
            jax.ShapeDtypeStruct((2, half_rows, CAP * tile), jnp.bfloat16),
            jax.ShapeDtypeStruct((2, FROWS, SLABS * FROWS), jnp.bfloat16),
            jax.ShapeDtypeStruct((SLABS, VT), jnp.int32),
        ] + [jax.ShapeDtypeStruct((OCC, CAP * tile, LANES), jnp.bfloat16)] * count,
        grid_spec=pltpu.PrefetchScalarGridSpec(
            num_scalar_prefetch=2,
            grid=(CAP,),
            in_specs=[
                pl.BlockSpec((tile, OCC, cols), lambda q, mask, ids: (tile_of(mask, ids[0], q), 0, 0)),
                half_block(0),
                half_block(1),
                pl.BlockSpec(occ_density.shape, lambda q, mask, ids: (0, 0)),
            ],
            out_specs=[
                pl.BlockSpec((2, half_rows, tile), lambda q, mask, ids: (0, 0, q)),
                pl.BlockSpec((2, FROWS, SLABS * FROWS), lambda q, mask, ids: (0, 0, 0)),
                pl.BlockSpec(memory_space=pltpu.SMEM),
            ] + [pl.BlockSpec((OCC, tile, LANES), lambda q, mask, ids: (0, q, 0))] * count,
        ),
        compiler_params=pltpu.CompilerParams(vmem_limit_bytes=VMEM),
        cost_estimate=pl.CostEstimate(flops=3 << 30, bytes_accessed=12 << 20, transcendentals=0),
    )(mask, ids, three_index, by_half, by_half, occ_density)
    return packs, virt, occ, table


def density_body(slabs, begins, ends, *refs):
    table_ref, ids_ref, *refs = refs
    count = len(slabs)
    sources, (virt_in, occ_in), refs = refs[:count], refs[count:count + 2], refs[count + 2:]
    if not begins:
        partial, *refs = refs
    out, packs, virt_ref, occ_ref, total, mixed, result, in_sems, out_sems = refs
    depth = sources[0].shape[1]
    half_rows = virt_ref.shape[1]
    blocks = half_rows // SPAN
    tile = depth // CAP
    targets = [packs.at[n, :, pl.ds(0, depth), :] for n in range(count)] + [virt_ref, occ_ref]
    arrivals = [
        pltpu.make_async_copy(ref, target, in_sems.at[n])
        for n, (ref, target) in enumerate(zip(list(sources) + [virt_in, occ_in], targets))
    ]
    if not begins:
        arrivals.append(pltpu.make_async_copy(partial, total, in_sems.at[count + 2]))
    for n in [0, count] + list(range(1, count)) + list(range(count + 1, len(arrivals))):
        arrivals[n].start()
    for n in range(count):
        packs[n, :, depth:depth + FINE, :] = jnp.zeros((OCC, FINE, LANES), jnp.bfloat16)
    perm = permutation(True) if ends else None
    waited = set()

    def arrived(n):
        if n not in waited:
            waited.add(n)
            arrivals[n].wait()

    arrived(count)
    if not begins:
        arrived(count + 2)
    for n, slab in enumerate(slabs):
        if slab >= 2:
            continue
        arrived(n)
        for i in range(0, OCC, 2):
            both = jnp.concatenate([packs[n, i, :depth], packs[n, i + 1, :depth]], axis=1)
            y = dot(virt_ref[slab], both)
            for j in range(2):
                part = y[:, j * LANES:(j + 1) * LANES]
                total[slab, i + j] = part if begins else part + total[slab, i + j]
    for n in range(len(arrivals)):
        arrived(n)
    fresh = [which for which in range(2) if begins and which not in slabs]
    departures = []
    for which in range(2):
        half = ids_ref[1] if which == 0 else 1 - ids_ref[1]
        weights = jnp.concatenate([occ_ref[which][:, s * FROWS:(s + 1) * FROWS] for s in slabs], axis=1)
        for first in range(0, half_rows, 2 * FINE):
            columns = []
            for row in (first, first + FINE):
                start = row // SPAN * (HALVES * SPAN) + row % SPAN + half * SPAN
                parts = []
                for n, s in enumerate(slabs):
                    base = table_ref[s, start // tile]
                    at = pl.multiple_of(jnp.where(base < 0, depth, base + start % tile), FINE)
                    parts.append(packs[n, :, pl.ds(at, FINE), :].reshape(FROWS, LANES))
                columns.append(jnp.concatenate(parts, axis=0))
            y = dot(weights, jnp.concatenate(columns, axis=1))
            for n in range(2):
                row = first + n * FINE
                part = y[:, n * LANES:(n + 1) * LANES].reshape(OCC, FINE, LANES)
                if which not in fresh:
                    part = part + total[which, :, row:row + FINE, :]
                if ends:
                    mixed[which, :, row:row + FINE, :] = part.astype(jnp.bfloat16)
                else:
                    total[which, :, row:row + FINE, :] = part
        if not ends:
            copy = pltpu.make_async_copy(total.at[which], out.at[which], out_sems.at[which])
            copy.start()
            departures.append(copy)
            continue
        for first in range(0, half_rows, 2 * GROUP):
            pair = transpose_rows(perm, [
                mixed[which, :, row:row + GROUP, :].reshape(ROWS, LANES) for row in (first, first + GROUP)
            ])
            for n in range(2):
                at = (first + n * GROUP) * OCC
                result[which, at:at + ROWS, :] = pair[n]
        for b in range(blocks):
            start = pl.multiple_of((b * HALVES + half) * SPAN * OCC, SPAN * OCC)
            copy = pltpu.make_async_copy(
                result.at[which, pl.ds(b * SPAN * OCC, SPAN * OCC), :],
                out.at[pl.ds(start, SPAN * OCC), :],
                out_sems.at[which * blocks + b],
            )
            copy.start()
            departures.append(copy)
    for copy in departures:
        copy.wait()


def density(table, ids, slabs, packs, virt, occ, partial=None, ends=True):
    depth = packs[0].shape[1]
    half_rows = virt.shape[1]
    rows = 2 * half_rows * OCC
    sums = (2, OCC, half_rows, LANES)
    begins = partial is None
    share = len(slabs) * LANES
    extra = [] if begins else [partial]
    return pl.pallas_call(
        functools.partial(density_body, slabs, begins, ends),
        out_shape=jax.ShapeDtypeStruct((rows, LANES), jnp.bfloat16) if ends else jax.ShapeDtypeStruct(sums, jnp.float32),
        grid_spec=pltpu.PrefetchScalarGridSpec(
            num_scalar_prefetch=2,
            grid=(1,),
            in_specs=[pl.BlockSpec(memory_space=pl.ANY)] * (len(slabs) + 2 + len(extra)),
            out_specs=pl.BlockSpec(memory_space=pl.ANY),
            scratch_shapes=[
                pltpu.VMEM((len(slabs), OCC, depth + FINE, LANES), jnp.bfloat16),
                pltpu.VMEM(virt.shape, jnp.bfloat16),
                pltpu.VMEM(occ.shape, jnp.bfloat16),
                pltpu.VMEM(sums, jnp.float32),
                pltpu.VMEM(sums if ends else (OCC, LANES), jnp.bfloat16),
                pltpu.VMEM((2, half_rows * OCC, LANES) if ends else (OCC, LANES), jnp.bfloat16),
                pltpu.SemaphoreType.DMA((len(slabs) + 3,)),
                pltpu.SemaphoreType.DMA((2 * half_rows // SPAN,)),
            ],
        ),
        compiler_params=pltpu.CompilerParams(vmem_limit_bytes=24 << 20),
        cost_estimate=pl.CostEstimate(
            flops=share * (rows * depth // 2 + 2 * rows * ROWS),
            bytes_accessed=share * OCC * depth * 2 + rows * LANES * 2,
            transcendentals=0,
        ),
    )(table, ids, *packs, virt, occ, *extra)


def assemble_body(*refs):
    count = len(refs) - 5
    ins, out = refs[:count], refs[count]
    arrived, whole, in_sems, out_sems = refs[count + 1:]
    rows = out.shape[0]
    peers = ins[0].shape[0] // rows
    cols = out.shape[2] // peers
    steps = peers // INNER

    def arrivals(n):
        part = pl.ds(pl.multiple_of(n * INNER * rows, INNER * rows), INNER * rows)
        return [
            pltpu.make_async_copy(ref.at[part], arrived.at[k, part], in_sems.at[n, k]) for k, ref in enumerate(ins)
        ]

    def departure(n):
        part = pl.ds(pl.multiple_of(n * INNER * cols, INNER * cols), INNER * cols)
        return pltpu.make_async_copy(whole.at[:, :, part], out.at[:, :, part], out_sems.at[n])

    def fetch(n, carry):
        for copy in arrivals(n):
            copy.start()
        return carry

    def place(n, carry):
        for copy in arrivals(n):
            copy.wait()
        for m in range(INNER):
            at = pl.multiple_of((n * INNER + m) * rows, rows)
            for k in range(count):
                first = pl.multiple_of((n * INNER + m) * cols + k * LANES, LANES)
                whole[:, :, pl.ds(first, LANES)] = arrived[k, pl.ds(at, rows)]
        departure(n).start()
        return carry

    def leave(n, carry):
        departure(n).wait()
        return carry

    lax.fori_loop(0, steps, fetch, 0)
    lax.fori_loop(0, steps, place, 0)
    lax.fori_loop(0, steps, leave, 0)


def assemble(parts, peers, cols):
    rows = parts[0].shape[0] // peers
    shape = (rows, OCC, peers * cols)
    return pl.pallas_call(
        assemble_body,
        out_shape=jax.ShapeDtypeStruct(shape, jnp.bfloat16),
        in_specs=[pl.BlockSpec(memory_space=pl.ANY)] * len(parts),
        out_specs=pl.BlockSpec(memory_space=pl.ANY),
        scratch_shapes=[
            pltpu.VMEM((len(parts),) + parts[0].shape, jnp.bfloat16),
            pltpu.VMEM(shape, jnp.bfloat16),
            pltpu.SemaphoreType.DMA((peers // INNER, len(parts))),
            pltpu.SemaphoreType.DMA((peers // INNER,)),
        ],
        compiler_params=pltpu.CompilerParams(vmem_limit_bytes=VMEM),
        cost_estimate=pl.CostEstimate(
            flops=0, bytes_accessed=4 * rows * OCC * shape[2], transcendentals=0
        ),
    )(*parts)


def place_body(part, _, out, held, in_sems, out_sems):
    rows = out.shape[0]
    peers = part.shape[0] // rows
    cols = out.shape[2] // peers
    steps = peers // INNER
    arrivals, departures = [], []
    for n in range(steps):
        some = pl.ds(n * INNER * rows, INNER * rows)
        copy = pltpu.make_async_copy(part.at[some], held.at[some], in_sems.at[n])
        copy.start()
        arrivals.append(copy)
    for n in range(steps):
        arrivals[n].wait()
        for m in range(n * INNER, (n + 1) * INNER):
            copy = pltpu.make_async_copy(
                held.at[pl.ds(m * rows, rows)],
                out.at[:, :, pl.ds((m + 1) * cols - LANES, LANES)],
                out_sems.at[m],
            )
            copy.start()
            departures.append(copy)
    for copy in departures:
        copy.wait()


def place_last(part, whole):
    peers = part.shape[0] // whole.shape[0]
    return pl.pallas_call(
        place_body,
        out_shape=jax.ShapeDtypeStruct(whole.shape, whole.dtype),
        in_specs=[pl.BlockSpec(memory_space=pl.ANY)] * 2,
        out_specs=pl.BlockSpec(memory_space=pl.ANY),
        scratch_shapes=[
            pltpu.VMEM(part.shape, jnp.bfloat16),
            pltpu.SemaphoreType.DMA((peers // INNER,)),
            pltpu.SemaphoreType.DMA((peers,)),
        ],
        input_output_aliases={1: 0},
        compiler_params=pltpu.CompilerParams(vmem_limit_bytes=VMEM),
        cost_estimate=pl.CostEstimate(flops=0, bytes_accessed=4 * part.size, transcendentals=0),
    )(part, whole)


def exchange_groups(peers):
    groups = []
    for parity in range(2):
        for core in range(2):
            groups.append([
                (2 * (((k // INNER) % HALVES) ^ parity) + core) * peers + k for k in range(peers)
            ])
    return groups


def local(three_index, tile_mask, occ_density, virt_density):
    virt_count = three_index.shape[0]
    peers = lax.axis_size("aux")
    own = lax.axis_index("occ")
    my_half = (lax.axis_index("aux") // INNER) % HALVES
    by_half = virt_density.reshape(peers // (HALVES * INNER), HALVES, -1, virt_count)

    head = first_pack(tile_mask, three_index)
    ids = jnp.stack(lax.optimization_barrier((own, my_half, head))[:2]).astype(jnp.int32)
    others, *weights = rest_pack(tile_mask, ids, three_index, by_half, occ_density)
    virt, occ, table = (pltpu.with_memory_space_constraint(array, pltpu.HBM) for array in weights)
    mine = [head] + others

    chip_pairs = [(s, s ^ 2) for s in range(SLABS)]
    core_pairs = [(s, s ^ 1) for s in range(SLABS)]
    groups = exchange_groups(peers)
    done, acrosses = [], []
    last = len(mine) - 1
    besides = [lax.ppermute(part, "occ", core_pairs) for part in mine]
    for k, part in enumerate(mine):
        sent = part
        if k >= 2:
            sent, _ = lax.optimization_barrier((part, acrosses[k - 2]))
        across = lax.ppermute(sent, "occ", chip_pairs)
        beside = besides[k]
        partial = None
        if k in (0, last):
            own_part = part if k == 0 else lax.optimization_barrier((part, gamma))[0]
            partial = density(table, ids, (0, 2), (own_part, beside), virt, occ, ends=False)
        before = (mine[1], partial, *besides[1:]) if k == 0 else (gamma, partial) if k == last else (gamma,)
        across, *before = lax.optimization_barrier((across,) + before)
        if k == 0:
            besides[1:] = before[2:]
        acrosses.append(across)
        diagonal = lax.ppermute(across, "occ", core_pairs)
        if partial is None:
            gamma = density(table, ids, (0, 1, 2, 3), (part, across, beside, diagonal), virt, occ)
        else:
            gamma = density(table, ids, (1, 3), (across, diagonal), virt, occ, partial=before[1])
        done.append(lax.all_to_all(
            gamma.reshape(virt_count, OCC, -1), ("occ", "aux"),
            split_axis=0, concat_axis=0, axis_index_groups=groups, tiled=True,
        ))
    return place_last(done[-1], assemble(done[:-1], peers, three_index.shape[2]))


def solution(mesh):
    return jax.shard_map(
        local,
        mesh=mesh,
        in_specs=(P(None, "occ", "aux"), P(), P(), P()),
        out_specs=P("aux", "occ", None),
        check_vma=False,
    )
```

```python
import functools

import jax
import jax.numpy as jnp
from jax import lax
from jax.experimental import pallas as pl
from jax.experimental.pallas import tpu as pltpu
from jax.sharding import PartitionSpec as P

VT = 6
CAP = 4
OCC = 8
SLABS = 4
FLIPS = (0, 2, 1, 3)
LANES = 128
GROUP = 32
ROWS = GROUP * OCC
FINE = 16
FROWS = FINE * OCC
HALVES = 2
SPAN = 96
INNER = 4
VMEM = 60 << 20


def iota(shape, dim):
    return lax.broadcasted_iota(jnp.int32, shape, dim)


def one_hot(condition):
    return jnp.where(condition, 1.0, 0.0).astype(jnp.bfloat16)


def dot(left, right):
    return jnp.dot(left, right, preferred_element_type=jnp.float32)


def permutation(back):
    shape = (ROWS, ROWS)
    fine, coarse = (iota(shape, 1), iota(shape, 0)) if back else (iota(shape, 0), iota(shape, 1))
    return one_hot((fine % GROUP == coarse // OCC) & (fine // GROUP == coarse % OCC))


def tile_of(mask_ref, slab, q):
    seen, tile = 0, 0
    for t in range(VT):
        seen = seen + mask_ref[slab, t]
        tile = tile + (seen <= q).astype(jnp.int32)
    return jnp.minimum(tile, VT - 1)


def transpose_rows(perm, columns):
    y = dot(perm, jnp.concatenate(columns, axis=1)).astype(jnp.bfloat16)
    return y[:, :LANES], y[:, LANES:]


def pack_rows(perm, x_ref, outs, first):
    for g in range(0, x_ref.shape[0] // GROUP, 2):
        for c, out in enumerate(outs):
            cols = slice((first + c) * LANES, (first + c + 1) * LANES)
            pair = transpose_rows(perm, [
                x_ref[n * GROUP:(n + 1) * GROUP, :, cols].reshape(ROWS, LANES) for n in (g, g + 1)
            ])
            for n in range(2):
                at = (g + n) * GROUP
                out[:, at:at + GROUP, :] = pair[n].reshape(OCC, GROUP, LANES)


def first_body(mask_ref, x_ref, out, tiles, packed, in_sems, out_sems):
    tile = tiles.shape[1]
    own = lax.axis_index("occ")
    arrivals, departures = [], []
    for q in range(CAP):
        at = pl.multiple_of(tile_of(mask_ref, own, q) * tile, tile)
        copy = pltpu.make_async_copy(x_ref.at[pl.ds(at, tile), :, pl.ds(0, LANES)], tiles.at[q], in_sems.at[q])
        copy.start()
        arrivals.append(copy)
    perm = permutation(False)
    for q in range(CAP):
        arrivals[q].wait()
        pack_rows(perm, tiles.at[q], [packed.at[q]], 0)
        copy = pltpu.make_async_copy(packed.at[q], out.at[:, pl.ds(q * tile, tile), :], out_sems.at[q])
        copy.start()
        departures.append(copy)
    for copy in departures:
        copy.wait()


def first_pack(mask, three_index):
    tile = three_index.shape[0] // VT
    return pl.pallas_call(
        first_body,
        out_shape=jax.ShapeDtypeStruct((OCC, CAP * tile, LANES), jnp.bfloat16),
        grid_spec=pltpu.PrefetchScalarGridSpec(
            num_scalar_prefetch=1,
            grid=(1,),
            in_specs=[pl.BlockSpec(memory_space=pl.ANY)],
            out_specs=pl.BlockSpec(memory_space=pl.ANY),
            scratch_shapes=[
                pltpu.VMEM((CAP, tile, OCC, LANES), jnp.bfloat16),
                pltpu.VMEM((CAP, OCC, tile, LANES), jnp.bfloat16),
                pltpu.SemaphoreType.DMA((CAP,)),
                pltpu.SemaphoreType.DMA((CAP,)),
            ],
        ),
        compiler_params=pltpu.CompilerParams(vmem_limit_bytes=VMEM),
        cost_estimate=pl.CostEstimate(flops=1 << 29, bytes_accessed=2 << 20, transcendentals=0),
    )(mask, three_index)


def rest_body(mask_ref, ids_ref, x_ref, v0_ref, v1_ref, d_ref, virt_out, occ_out, table_out, *outs):
    q = pl.program_id(0)
    own = ids_ref[0]
    pack_rows(permutation(False), x_ref, outs, 1)
    for which, v_ref in enumerate((v0_ref, v1_ref)):
        count = 0
        for t in range(VT):
            count = count + mask_ref[own ^ FLIPS[which], t]
        part = v_ref[...].reshape(-1, x_ref.shape[0])
        virt_out[which] = jnp.where(q < count, part, jnp.zeros_like(part))

    @pl.when(q == 0)
    def _():
        tile = x_ref.shape[0]
        for s in range(SLABS):
            seen = 0
            for t in range(VT):
                here = mask_ref[own ^ FLIPS[s], t]
                table_out[s, t] = jnp.where(here > 0, seen * tile, -1)
                seen = seen + here
        width = SLABS * FROWS
        shape = (SLABS * OCC, width)
        col = iota(shape, 1)
        slab = col // FROWS
        source = own
        for s in range(1, SLABS):
            source = jnp.where(slab == s, own ^ FLIPS[s], source)
        pick_cols = one_hot(iota(shape, 0) == source * OCC + col % FROWS // FINE)
        spread = dot(d_ref[...], pick_cols).astype(jnp.bfloat16)
        shape = (FROWS, SLABS * OCC)
        full = (FROWS, width)
        same = iota(full, 0) % FINE == iota(full, 1) % FINE
        for which in range(2):
            pick_rows = one_hot(iota(shape, 1) == (own ^ FLIPS[which]) * OCC + iota(shape, 0) // FINE)
            occ_out[which] = jnp.where(same, dot(pick_rows, spread), 0.0).astype(jnp.bfloat16)


def rest_pack(mask, ids, three_index, by_half, occ_density):
    virt_count, _, cols = three_index.shape
    tile = virt_count // VT
    blocks, _, span, _ = by_half.shape
    half_rows = blocks * span
    count = cols // LANES - 1

    def half_block(which):
        def index(q, mask, ids):
            half = ids[1] if which == 0 else 1 - ids[1]
            return 0, half, 0, tile_of(mask, ids[0] ^ FLIPS[which], q)
        return pl.BlockSpec((blocks, 1, span, tile), index)

    virt, occ, table, *packs = pl.pallas_call(
        rest_body,
        out_shape=[
            jax.ShapeDtypeStruct((2, half_rows, CAP * tile), jnp.bfloat16),
            jax.ShapeDtypeStruct((2, FROWS, SLABS * FROWS), jnp.bfloat16),
            jax.ShapeDtypeStruct((SLABS, VT), jnp.int32),
        ] + [jax.ShapeDtypeStruct((OCC, CAP * tile, LANES), jnp.bfloat16)] * count,
        grid_spec=pltpu.PrefetchScalarGridSpec(
            num_scalar_prefetch=2,
            grid=(CAP,),
            in_specs=[
                pl.BlockSpec((tile, OCC, cols), lambda q, mask, ids: (tile_of(mask, ids[0], q), 0, 0)),
                half_block(0),
                half_block(1),
                pl.BlockSpec(occ_density.shape, lambda q, mask, ids: (0, 0)),
            ],
            out_specs=[
                pl.BlockSpec((2, half_rows, tile), lambda q, mask, ids: (0, 0, q)),
                pl.BlockSpec((2, FROWS, SLABS * FROWS), lambda q, mask, ids: (0, 0, 0)),
                pl.BlockSpec(memory_space=pltpu.SMEM),
            ] + [pl.BlockSpec((OCC, tile, LANES), lambda q, mask, ids: (0, q, 0))] * count,
        ),
        compiler_params=pltpu.CompilerParams(vmem_limit_bytes=VMEM),
        cost_estimate=pl.CostEstimate(flops=3 << 30, bytes_accessed=12 << 20, transcendentals=0),
    )(mask, ids, three_index, by_half, by_half, occ_density)
    return packs, virt, occ, table


def density_body(slabs, begins, ends, *refs):
    table_ref, ids_ref, *refs = refs
    count = len(slabs)
    sources, (virt_in, occ_in), refs = refs[:count], refs[count:count + 2], refs[count + 2:]
    if not begins:
        partial, *refs = refs
    out, packs, virt_ref, occ_ref, total, mixed, result, in_sems, out_sems = refs
    depth = sources[0].shape[1]
    half_rows = virt_ref.shape[1]
    blocks = half_rows // SPAN
    tile = depth // CAP
    targets = [packs.at[n, :, pl.ds(0, depth), :] for n in range(count)] + [virt_ref, occ_ref]
    arrivals = [
        pltpu.make_async_copy(ref, target, in_sems.at[n])
        for n, (ref, target) in enumerate(zip(list(sources) + [virt_in, occ_in], targets))
    ]
    if not begins:
        arrivals.append(pltpu.make_async_copy(partial, total, in_sems.at[count + 2]))
    for n in [0, count] + list(range(1, count)) + list(range(count + 1, len(arrivals))):
        arrivals[n].start()
    for n in range(count):
        packs[n, :, depth:depth + FINE, :] = jnp.zeros((OCC, FINE, LANES), jnp.bfloat16)
    perm = permutation(True) if ends else None
    waited = set()

    def arrived(n):
        if n not in waited:
            waited.add(n)
            arrivals[n].wait()

    arrived(count)
    if not begins:
        arrived(count + 2)
    for n, slab in enumerate(slabs):
        if slab >= 2:
            continue
        arrived(n)
        for i in range(0, OCC, 2):
            both = jnp.concatenate([packs[n, i, :depth], packs[n, i + 1, :depth]], axis=1)
            y = dot(virt_ref[slab], both)
            for j in range(2):
                part = y[:, j * LANES:(j + 1) * LANES]
                total[slab, i + j] = part if begins else part + total[slab, i + j]
    for n in range(len(arrivals)):
        arrived(n)
    fresh = [which for which in range(2) if begins and which not in slabs]
    departures = []
    for which in range(2):
        half = ids_ref[1] if which == 0 else 1 - ids_ref[1]
        weights = jnp.concatenate([occ_ref[which][:, s * FROWS:(s + 1) * FROWS] for s in slabs], axis=1)
        for first in range(0, half_rows, 2 * FINE):
            columns = []
            for row in (first, first + FINE):
                start = row // SPAN * (HALVES * SPAN) + row % SPAN + half * SPAN
                parts = []
                for n, s in enumerate(slabs):
                    base = table_ref[s, start // tile]
                    at = pl.multiple_of(jnp.where(base < 0, depth, base + start % tile), FINE)
                    parts.append(packs[n, :, pl.ds(at, FINE), :].reshape(FROWS, LANES))
                columns.append(jnp.concatenate(parts, axis=0))
            y = dot(weights, jnp.concatenate(columns, axis=1))
            for n in range(2):
                row = first + n * FINE
                part = y[:, n * LANES:(n + 1) * LANES].reshape(OCC, FINE, LANES)
                if which not in fresh:
                    part = part + total[which, :, row:row + FINE, :]
                if ends:
                    mixed[which, :, row:row + FINE, :] = part.astype(jnp.bfloat16)
                else:
                    total[which, :, row:row + FINE, :] = part
        if not ends:
            copy = pltpu.make_async_copy(total.at[which], out.at[which], out_sems.at[which])
            copy.start()
            departures.append(copy)
            continue
        for first in range(0, half_rows, 2 * GROUP):
            pair = transpose_rows(perm, [
                mixed[which, :, row:row + GROUP, :].reshape(ROWS, LANES) for row in (first, first + GROUP)
            ])
            for n in range(2):
                at = (first + n * GROUP) * OCC
                result[which, at:at + ROWS, :] = pair[n]
        for b in range(blocks):
            start = pl.multiple_of((b * HALVES + half) * SPAN * OCC, SPAN * OCC)
            copy = pltpu.make_async_copy(
                result.at[which, pl.ds(b * SPAN * OCC, SPAN * OCC), :],
                out.at[pl.ds(start, SPAN * OCC), :],
                out_sems.at[which * blocks + b],
            )
            copy.start()
            departures.append(copy)
    for copy in departures:
        copy.wait()


def density(table, ids, slabs, packs, virt, occ, partial=None, ends=True):
    depth = packs[0].shape[1]
    half_rows = virt.shape[1]
    rows = 2 * half_rows * OCC
    sums = (2, OCC, half_rows, LANES)
    begins = partial is None
    share = len(slabs) * LANES
    extra = [] if begins else [partial]
    return pl.pallas_call(
        functools.partial(density_body, slabs, begins, ends),
        out_shape=jax.ShapeDtypeStruct((rows, LANES), jnp.bfloat16) if ends else jax.ShapeDtypeStruct(sums, jnp.float32),
        grid_spec=pltpu.PrefetchScalarGridSpec(
            num_scalar_prefetch=2,
            grid=(1,),
            in_specs=[pl.BlockSpec(memory_space=pl.ANY)] * (len(slabs) + 2 + len(extra)),
            out_specs=pl.BlockSpec(memory_space=pl.ANY),
            scratch_shapes=[
                pltpu.VMEM((len(slabs), OCC, depth + FINE, LANES), jnp.bfloat16),
                pltpu.VMEM(virt.shape, jnp.bfloat16),
                pltpu.VMEM(occ.shape, jnp.bfloat16),
                pltpu.VMEM(sums, jnp.float32),
                pltpu.VMEM(sums if ends else (OCC, LANES), jnp.bfloat16),
                pltpu.VMEM((2, half_rows * OCC, LANES) if ends else (OCC, LANES), jnp.bfloat16),
                pltpu.SemaphoreType.DMA((len(slabs) + 3,)),
                pltpu.SemaphoreType.DMA((2 * half_rows // SPAN,)),
            ],
        ),
        compiler_params=pltpu.CompilerParams(vmem_limit_bytes=24 << 20),
        cost_estimate=pl.CostEstimate(
            flops=share * (rows * depth // 2 + 2 * rows * ROWS),
            bytes_accessed=share * OCC * depth * 2 + rows * LANES * 2,
            transcendentals=0,
        ),
    )(table, ids, *packs, virt, occ, *extra)


def assemble_body(*refs):
    count = len(refs) - 5
    ins, out = refs[:count], refs[count]
    arrived, whole, in_sems, out_sems = refs[count + 1:]
    rows = out.shape[0]
    peers = ins[0].shape[0] // rows
    cols = out.shape[2] // peers
    steps = peers // INNER

    def arrivals(n):
        part = pl.ds(pl.multiple_of(n * INNER * rows, INNER * rows), INNER * rows)
        return [
            pltpu.make_async_copy(ref.at[part], arrived.at[k, part], in_sems.at[n, k]) for k, ref in enumerate(ins)
        ]

    def departure(n):
        part = pl.ds(pl.multiple_of(n * INNER * cols, INNER * cols), INNER * cols)
        return pltpu.make_async_copy(whole.at[:, :, part], out.at[:, :, part], out_sems.at[n])

    def fetch(n, carry):
        for copy in arrivals(n):
            copy.start()
        return carry

    def place(n, carry):
        for copy in arrivals(n):
            copy.wait()
        for m in range(INNER):
            at = pl.multiple_of((n * INNER + m) * rows, rows)
            for k in range(count):
                first = pl.multiple_of((n * INNER + m) * cols + k * LANES, LANES)
                whole[:, :, pl.ds(first, LANES)] = arrived[k, pl.ds(at, rows)]
        departure(n).start()
        return carry

    def leave(n, carry):
        departure(n).wait()
        return carry

    lax.fori_loop(0, steps, fetch, 0)
    lax.fori_loop(0, steps, place, 0)
    lax.fori_loop(0, steps, leave, 0)


def assemble(parts, peers, cols):
    rows = parts[0].shape[0] // peers
    shape = (rows, OCC, peers * cols)
    return pl.pallas_call(
        assemble_body,
        out_shape=jax.ShapeDtypeStruct(shape, jnp.bfloat16),
        in_specs=[pl.BlockSpec(memory_space=pl.ANY)] * len(parts),
        out_specs=pl.BlockSpec(memory_space=pl.ANY),
        scratch_shapes=[
            pltpu.VMEM((len(parts),) + parts[0].shape, jnp.bfloat16),
            pltpu.VMEM(shape, jnp.bfloat16),
            pltpu.SemaphoreType.DMA((peers // INNER, len(parts))),
            pltpu.SemaphoreType.DMA((peers // INNER,)),
        ],
        compiler_params=pltpu.CompilerParams(vmem_limit_bytes=VMEM),
        cost_estimate=pl.CostEstimate(
            flops=0, bytes_accessed=4 * rows * OCC * shape[2], transcendentals=0
        ),
    )(*parts)


def place_body(part, _, out, sems):
    rows = out.shape[0]
    peers = part.shape[0] // rows
    cols = out.shape[2] // peers
    copies = []
    for m in range(peers):
        copy = pltpu.make_async_copy(
            part.at[pl.ds(m * rows, rows)],
            out.at[:, :, pl.ds((m + 1) * cols - LANES, LANES)],
            sems.at[m],
        )
        copy.start()
        copies.append(copy)
    for copy in copies:
        copy.wait()


def place_last(part, whole):
    peers = part.shape[0] // whole.shape[0]
    return pl.pallas_call(
        place_body,
        out_shape=jax.ShapeDtypeStruct(whole.shape, whole.dtype),
        in_specs=[pl.BlockSpec(memory_space=pltpu.VMEM), pl.BlockSpec(memory_space=pl.ANY)],
        out_specs=pl.BlockSpec(memory_space=pl.ANY),
        scratch_shapes=[pltpu.SemaphoreType.DMA((peers,))],
        input_output_aliases={1: 0},
        compiler_params=pltpu.CompilerParams(vmem_limit_bytes=8 << 20),
        cost_estimate=pl.CostEstimate(flops=0, bytes_accessed=4 * part.size, transcendentals=0),
    )(part, whole)


def exchange_groups(peers):
    groups = []
    for parity in range(2):
        for core in range(2):
            groups.append([
                (2 * (((k // INNER) % HALVES) ^ parity) + core) * peers + k for k in range(peers)
            ])
    return groups


def local(three_index, tile_mask, occ_density, virt_density):
    virt_count = three_index.shape[0]
    peers = lax.axis_size("aux")
    own = lax.axis_index("occ")
    my_half = (lax.axis_index("aux") // INNER) % HALVES
    by_half = virt_density.reshape(peers // (HALVES * INNER), HALVES, -1, virt_count)

    head = first_pack(tile_mask, three_index)
    ids = jnp.stack(lax.optimization_barrier((own, my_half, head))[:2]).astype(jnp.int32)
    others, *weights = rest_pack(tile_mask, ids, three_index, by_half, occ_density)
    virt, occ, table = (pltpu.with_memory_space_constraint(array, pltpu.HBM) for array in weights)
    mine = [head] + others

    chip_pairs = [(s, s ^ 2) for s in range(SLABS)]
    core_pairs = [(s, s ^ 1) for s in range(SLABS)]
    groups = exchange_groups(peers)
    done, acrosses = [], []
    last = len(mine) - 1
    besides = [lax.ppermute(part, "occ", core_pairs) for part in mine]
    for k, part in enumerate(mine):
        sent = part
        if k >= 2:
            sent, _ = lax.optimization_barrier((part, acrosses[k - 2]))
        across = lax.ppermute(sent, "occ", chip_pairs)
        beside = besides[k]
        partial = None
        if k in (0, last):
            own_part = part if k == 0 else lax.optimization_barrier((part, gamma))[0]
            partial = density(table, ids, (0, 2), (own_part, beside), virt, occ, ends=False)
        before = (mine[1], partial) if k == 0 else (gamma, partial) if k == last else (gamma,)
        across, *before = lax.optimization_barrier((across,) + before)
        acrosses.append(across)
        diagonal = lax.ppermute(across, "occ", core_pairs)
        if partial is None:
            gamma = density(table, ids, (0, 1, 2, 3), (part, across, beside, diagonal), virt, occ)
        else:
            gamma = density(table, ids, (1, 3), (across, diagonal), virt, occ, partial=before[1])
        done.append(lax.all_to_all(
            gamma.reshape(virt_count, OCC, -1), ("occ", "aux"),
            split_axis=0, concat_axis=0, axis_index_groups=groups, tiled=True,
        ))
    return place_last(done[-1], assemble(done[:-1], peers, three_index.shape[2]))


def solution(mesh):
    return jax.shard_map(
        local,
        mesh=mesh,
        in_specs=(P(None, "occ", "aux"), P(), P(), P()),
        out_specs=P("aux", "occ", None),
        check_vma=False,
    )
```

```python
import functools

import jax
import jax.numpy as jnp
from jax import lax
from jax.experimental import pallas as pl
from jax.experimental.pallas import tpu as pltpu
from jax.sharding import PartitionSpec as P

VT = 6
CAP = 4
OCC = 8
SLABS = 4
FLIPS = (0, 2, 1, 3)
LANES = 128
GROUP = 32
ROWS = GROUP * OCC
FINE = 16
FROWS = FINE * OCC
HALVES = 2
SPAN = 96
INNER = 4
VMEM = 60 << 20


def iota(shape, dim):
    return lax.broadcasted_iota(jnp.int32, shape, dim)


def one_hot(condition):
    return jnp.where(condition, 1.0, 0.0).astype(jnp.bfloat16)


def dot(left, right):
    return jnp.dot(left, right, preferred_element_type=jnp.float32)


def permutation(back):
    shape = (ROWS, ROWS)
    fine, coarse = (iota(shape, 1), iota(shape, 0)) if back else (iota(shape, 0), iota(shape, 1))
    return one_hot((fine % GROUP == coarse // OCC) & (fine // GROUP == coarse % OCC))


def tile_of(mask_ref, slab, q):
    seen, tile = 0, 0
    for t in range(VT):
        seen = seen + mask_ref[slab, t]
        tile = tile + (seen <= q).astype(jnp.int32)
    return jnp.minimum(tile, VT - 1)


def transpose_rows(perm, columns):
    y = dot(perm, jnp.concatenate(columns, axis=1)).astype(jnp.bfloat16)
    return y[:, :LANES], y[:, LANES:]


def pack_rows(perm, x_ref, outs, first):
    for g in range(0, x_ref.shape[0] // GROUP, 2):
        for c, out in enumerate(outs):
            cols = slice((first + c) * LANES, (first + c + 1) * LANES)
            pair = transpose_rows(perm, [
                x_ref[n * GROUP:(n + 1) * GROUP, :, cols].reshape(ROWS, LANES) for n in (g, g + 1)
            ])
            for n in range(2):
                at = (g + n) * GROUP
                out[:, at:at + GROUP, :] = pair[n].reshape(OCC, GROUP, LANES)


def first_body(mask_ref, x_ref, out, tiles, packed, in_sems, out_sems):
    tile = tiles.shape[1]
    own = lax.axis_index("occ")
    arrivals, departures = [], []
    half = tile // 2
    for q in range(CAP):
        at = tile_of(mask_ref, own, q) * tile
        for n in range(2):
            rows = pl.ds(pl.multiple_of(at + n * half, half), half)
            copy = pltpu.make_async_copy(
                x_ref.at[rows, :, pl.ds(0, LANES)], tiles.at[q, pl.ds(n * half, half)], in_sems.at[2 * q + n]
            )
            copy.start()
            arrivals.append(copy)
    perm = permutation(False)
    for q in range(CAP):
        arrivals[2 * q].wait()
        arrivals[2 * q + 1].wait()
        pack_rows(perm, tiles.at[q], [packed.at[q]], 0)
        copy = pltpu.make_async_copy(packed.at[q], out.at[:, pl.ds(q * tile, tile), :], out_sems.at[q])
        copy.start()
        departures.append(copy)
    for copy in departures:
        copy.wait()


def first_pack(mask, three_index):
    tile = three_index.shape[0] // VT
    return pl.pallas_call(
        first_body,
        out_shape=jax.ShapeDtypeStruct((OCC, CAP * tile, LANES), jnp.bfloat16),
        grid_spec=pltpu.PrefetchScalarGridSpec(
            num_scalar_prefetch=1,
            grid=(1,),
            in_specs=[pl.BlockSpec(memory_space=pl.ANY)],
            out_specs=pl.BlockSpec(memory_space=pl.ANY),
            scratch_shapes=[
                pltpu.VMEM((CAP, tile, OCC, LANES), jnp.bfloat16),
                pltpu.VMEM((CAP, OCC, tile, LANES), jnp.bfloat16),
                pltpu.SemaphoreType.DMA((2 * CAP,)),
                pltpu.SemaphoreType.DMA((CAP,)),
            ],
        ),
        compiler_params=pltpu.CompilerParams(vmem_limit_bytes=VMEM),
        cost_estimate=pl.CostEstimate(flops=1 << 29, bytes_accessed=2 << 20, transcendentals=0),
    )(mask, three_index)


def rest_body(mask_ref, ids_ref, x_ref, v0_ref, v1_ref, d_ref, virt_out, occ_out, table_out, *outs):
    q = pl.program_id(0)
    own = ids_ref[0]
    pack_rows(permutation(False), x_ref, outs, 1)
    for which, v_ref in enumerate((v0_ref, v1_ref)):
        count = 0
        for t in range(VT):
            count = count + mask_ref[own ^ FLIPS[which], t]
        part = v_ref[...].reshape(-1, x_ref.shape[0])
        virt_out[which] = jnp.where(q < count, part, jnp.zeros_like(part))

    @pl.when(q == 0)
    def _():
        tile = x_ref.shape[0]
        for s in range(SLABS):
            seen = 0
            for t in range(VT):
                here = mask_ref[own ^ FLIPS[s], t]
                table_out[s, t] = jnp.where(here > 0, seen * tile, -1)
                seen = seen + here
        width = SLABS * FROWS
        shape = (SLABS * OCC, width)
        col = iota(shape, 1)
        slab = col // FROWS
        source = own
        for s in range(1, SLABS):
            source = jnp.where(slab == s, own ^ FLIPS[s], source)
        pick_cols = one_hot(iota(shape, 0) == source * OCC + col % FROWS // FINE)
        spread = dot(d_ref[...], pick_cols).astype(jnp.bfloat16)
        shape = (FROWS, SLABS * OCC)
        full = (FROWS, width)
        same = iota(full, 0) % FINE == iota(full, 1) % FINE
        for which in range(2):
            pick_rows = one_hot(iota(shape, 1) == (own ^ FLIPS[which]) * OCC + iota(shape, 0) // FINE)
            occ_out[which] = jnp.where(same, dot(pick_rows, spread), 0.0).astype(jnp.bfloat16)


def rest_pack(mask, ids, three_index, by_half, occ_density):
    virt_count, _, cols = three_index.shape
    tile = virt_count // VT
    blocks, _, span, _ = by_half.shape
    half_rows = blocks * span
    count = cols // LANES - 1

    def half_block(which):
        def index(q, mask, ids):
            half = ids[1] if which == 0 else 1 - ids[1]
            return 0, half, 0, tile_of(mask, ids[0] ^ FLIPS[which], q)
        return pl.BlockSpec((blocks, 1, span, tile), index)

    virt, occ, table, *packs = pl.pallas_call(
        rest_body,
        out_shape=[
            jax.ShapeDtypeStruct((2, half_rows, CAP * tile), jnp.bfloat16),
            jax.ShapeDtypeStruct((2, FROWS, SLABS * FROWS), jnp.bfloat16),
            jax.ShapeDtypeStruct((SLABS, VT), jnp.int32),
        ] + [jax.ShapeDtypeStruct((OCC, CAP * tile, LANES), jnp.bfloat16)] * count,
        grid_spec=pltpu.PrefetchScalarGridSpec(
            num_scalar_prefetch=2,
            grid=(CAP,),
            in_specs=[
                pl.BlockSpec((tile, OCC, cols), lambda q, mask, ids: (tile_of(mask, ids[0], q), 0, 0)),
                half_block(0),
                half_block(1),
                pl.BlockSpec(occ_density.shape, lambda q, mask, ids: (0, 0)),
            ],
            out_specs=[
                pl.BlockSpec((2, half_rows, tile), lambda q, mask, ids: (0, 0, q)),
                pl.BlockSpec((2, FROWS, SLABS * FROWS), lambda q, mask, ids: (0, 0, 0)),
                pl.BlockSpec(memory_space=pltpu.SMEM),
            ] + [pl.BlockSpec((OCC, tile, LANES), lambda q, mask, ids: (0, q, 0))] * count,
        ),
        compiler_params=pltpu.CompilerParams(vmem_limit_bytes=VMEM),
        cost_estimate=pl.CostEstimate(flops=3 << 30, bytes_accessed=12 << 20, transcendentals=0),
    )(mask, ids, three_index, by_half, by_half, occ_density)
    return packs, virt, occ, table


def density_body(slabs, begins, ends, only, *refs):
    if only is None:
        density_terms(slabs, begins, ends, *refs)
    else:
        @pl.when(refs[1][0] % 2 == only)
        def _():
            density_terms(slabs, begins, ends, *refs)


def density_terms(slabs, begins, ends, *refs):
    table_ref, ids_ref, *refs = refs
    count = len(slabs)
    sources, (virt_in, occ_in), refs = refs[:count], refs[count:count + 2], refs[count + 2:]
    partial = refs[0]
    out, packs, virt_ref, occ_ref, total, mixed, result, in_sems, out_sems = refs[-9:]
    depth = sources[0].shape[1]
    half_rows = virt_ref.shape[1]
    blocks = half_rows // SPAN
    tile = depth // CAP
    targets = [packs.at[n, :, pl.ds(0, depth), :] for n in range(count)] + [virt_ref, occ_ref]
    arrivals = [
        pltpu.make_async_copy(ref, target, in_sems.at[n])
        for n, (ref, target) in enumerate(zip(list(sources) + [virt_in, occ_in], targets))
    ]
    if not begins:
        arrivals.append(pltpu.make_async_copy(partial, total, in_sems.at[count + 2]))
    for n in [0, count] + list(range(1, count)) + list(range(count + 1, len(arrivals))):
        arrivals[n].start()
    for n in range(count):
        packs[n, :, depth:depth + FINE, :] = jnp.zeros((OCC, FINE, LANES), jnp.bfloat16)
    perm = permutation(True) if ends else None
    waited = set()

    def arrived(n):
        if n not in waited:
            waited.add(n)
            arrivals[n].wait()

    arrived(count)
    if not begins:
        arrived(count + 2)
    for n, slab in enumerate(slabs):
        if slab >= 2:
            continue
        arrived(n)
        for i in range(0, OCC, 2):
            both = jnp.concatenate([packs[n, i, :depth], packs[n, i + 1, :depth]], axis=1)
            y = dot(virt_ref[slab], both)
            for j in range(2):
                part = y[:, j * LANES:(j + 1) * LANES]
                total[slab, i + j] = part if begins else part + total[slab, i + j]
    for n in range(len(arrivals)):
        arrived(n)
    fresh = [which for which in range(2) if begins and which not in slabs]
    departures = []
    for which in range(2):
        half = ids_ref[1] if which == 0 else 1 - ids_ref[1]
        weights = jnp.concatenate([occ_ref[which][:, s * FROWS:(s + 1) * FROWS] for s in slabs], axis=1)
        for first in range(0, half_rows, 2 * FINE):
            columns = []
            for row in (first, first + FINE):
                start = row // SPAN * (HALVES * SPAN) + row % SPAN + half * SPAN
                parts = []
                for n, s in enumerate(slabs):
                    base = table_ref[s, start // tile]
                    at = pl.multiple_of(jnp.where(base < 0, depth, base + start % tile), FINE)
                    parts.append(packs[n, :, pl.ds(at, FINE), :].reshape(FROWS, LANES))
                columns.append(jnp.concatenate(parts, axis=0))
            y = dot(weights, jnp.concatenate(columns, axis=1))
            for n in range(2):
                row = first + n * FINE
                part = y[:, n * LANES:(n + 1) * LANES].reshape(OCC, FINE, LANES)
                if which not in fresh:
                    part = part + total[which, :, row:row + FINE, :]
                if ends:
                    mixed[which, :, row:row + FINE, :] = part.astype(jnp.bfloat16)
                else:
                    total[which, :, row:row + FINE, :] = part
        if not ends:
            copy = pltpu.make_async_copy(total.at[which], out.at[which], out_sems.at[which])
            copy.start()
            departures.append(copy)
            continue
        for first in range(0, half_rows, 2 * GROUP):
            pair = transpose_rows(perm, [
                mixed[which, :, row:row + GROUP, :].reshape(ROWS, LANES) for row in (first, first + GROUP)
            ])
            for n in range(2):
                at = (first + n * GROUP) * OCC
                result[which, at:at + ROWS, :] = pair[n]
        for b in range(blocks):
            start = pl.multiple_of((b * HALVES + half) * SPAN * OCC, SPAN * OCC)
            copy = pltpu.make_async_copy(
                result.at[which, pl.ds(b * SPAN * OCC, SPAN * OCC), :],
                out.at[pl.ds(start, SPAN * OCC), :],
                out_sems.at[which * blocks + b],
            )
            copy.start()
            departures.append(copy)
    for copy in departures:
        copy.wait()


def density(table, ids, slabs, packs, virt, occ, partial=None, ends=True, only=None, into=None):
    depth = packs[0].shape[1]
    half_rows = virt.shape[1]
    rows = 2 * half_rows * OCC
    sums = (2, OCC, half_rows, LANES)
    begins = partial is None
    share = len(slabs) * LANES
    extra = [array for array in (partial, into) if array is not None]
    aliases = {} if into is None else {2 + len(slabs) + 2: 0}
    return pl.pallas_call(
        functools.partial(density_body, slabs, begins, ends, only),
        out_shape=jax.ShapeDtypeStruct((rows, LANES), jnp.bfloat16) if ends else jax.ShapeDtypeStruct(sums, jnp.float32),
        grid_spec=pltpu.PrefetchScalarGridSpec(
            num_scalar_prefetch=2,
            grid=(1,),
            in_specs=[pl.BlockSpec(memory_space=pl.ANY)] * (len(slabs) + 2 + len(extra)),
            out_specs=pl.BlockSpec(memory_space=pl.ANY),
            scratch_shapes=[
                pltpu.VMEM((len(slabs), OCC, depth + FINE, LANES), jnp.bfloat16),
                pltpu.VMEM(virt.shape, jnp.bfloat16),
                pltpu.VMEM(occ.shape, jnp.bfloat16),
                pltpu.VMEM(sums, jnp.float32),
                pltpu.VMEM(sums if ends else (OCC, LANES), jnp.bfloat16),
                pltpu.VMEM((2, half_rows * OCC, LANES) if ends else (OCC, LANES), jnp.bfloat16),
                pltpu.SemaphoreType.DMA((len(slabs) + 3,)),
                pltpu.SemaphoreType.DMA((2 * half_rows // SPAN,)),
            ],
        ),
        input_output_aliases=aliases,
        compiler_params=pltpu.CompilerParams(vmem_limit_bytes=24 << 20),
        cost_estimate=pl.CostEstimate(
            flops=share * (rows * depth // 2 + 2 * rows * ROWS),
            bytes_accessed=share * OCC * depth * 2 + rows * LANES * 2,
            transcendentals=0,
        ),
    )(table, ids, *packs, virt, occ, *extra)


def assemble_body(*refs):
    count = len(refs) - 5
    ins, out = refs[:count], refs[count]
    arrived, whole, in_sems, out_sems = refs[count + 1:]
    rows = out.shape[0]
    peers = ins[0].shape[0] // rows
    cols = out.shape[2] // peers
    steps = peers // INNER

    def arrivals(n):
        part = pl.ds(pl.multiple_of(n * INNER * rows, INNER * rows), INNER * rows)
        return [
            pltpu.make_async_copy(ref.at[part], arrived.at[k, part], in_sems.at[n, k]) for k, ref in enumerate(ins)
        ]

    def departure(n):
        part = pl.ds(pl.multiple_of(n * INNER * cols, INNER * cols), INNER * cols)
        return pltpu.make_async_copy(whole.at[:, :, part], out.at[:, :, part], out_sems.at[n])

    def fetch(n, carry):
        for copy in arrivals(n):
            copy.start()
        return carry

    def place(n, carry):
        for copy in arrivals(n):
            copy.wait()
        for m in range(INNER):
            at = pl.multiple_of((n * INNER + m) * rows, rows)
            for k in range(count):
                first = pl.multiple_of((n * INNER + m) * cols + k * LANES, LANES)
                whole[:, :, pl.ds(first, LANES)] = arrived[k, pl.ds(at, rows)]
        departure(n).start()
        return carry

    def leave(n, carry):
        departure(n).wait()
        return carry

    lax.fori_loop(0, steps, fetch, 0)
    lax.fori_loop(0, steps, place, 0)
    lax.fori_loop(0, steps, leave, 0)


def assemble(parts, peers, cols):
    rows = parts[0].shape[0] // peers
    shape = (rows, OCC, peers * cols)
    return pl.pallas_call(
        assemble_body,
        out_shape=jax.ShapeDtypeStruct(shape, jnp.bfloat16),
        in_specs=[pl.BlockSpec(memory_space=pl.ANY)] * len(parts),
        out_specs=pl.BlockSpec(memory_space=pl.ANY),
        scratch_shapes=[
            pltpu.VMEM((len(parts),) + parts[0].shape, jnp.bfloat16),
            pltpu.VMEM(shape, jnp.bfloat16),
            pltpu.SemaphoreType.DMA((peers // INNER, len(parts))),
            pltpu.SemaphoreType.DMA((peers // INNER,)),
        ],
        compiler_params=pltpu.CompilerParams(vmem_limit_bytes=VMEM),
        cost_estimate=pl.CostEstimate(
            flops=0, bytes_accessed=4 * rows * OCC * shape[2], transcendentals=0
        ),
    )(*parts)


def place_body(part, _, out, sems):
    rows = out.shape[0]
    peers = part.shape[0] // rows
    cols = out.shape[2] // peers
    copies = []
    for m in range(peers):
        copy = pltpu.make_async_copy(
            part.at[pl.ds(m * rows, rows)],
            out.at[:, :, pl.ds((m + 1) * cols - LANES, LANES)],
            sems.at[m],
        )
        copy.start()
        copies.append(copy)
    for copy in copies:
        copy.wait()


def place_last(part, whole):
    peers = part.shape[0] // whole.shape[0]
    return pl.pallas_call(
        place_body,
        out_shape=jax.ShapeDtypeStruct(whole.shape, whole.dtype),
        in_specs=[pl.BlockSpec(memory_space=pltpu.VMEM), pl.BlockSpec(memory_space=pl.ANY)],
        out_specs=pl.BlockSpec(memory_space=pl.ANY),
        scratch_shapes=[pltpu.SemaphoreType.DMA((peers,))],
        input_output_aliases={1: 0},
        compiler_params=pltpu.CompilerParams(vmem_limit_bytes=8 << 20),
        cost_estimate=pl.CostEstimate(flops=0, bytes_accessed=4 * part.size, transcendentals=0),
    )(part, whole)


def exchange_groups(peers):
    groups = []
    for parity in range(2):
        for core in range(2):
            groups.append([
                (2 * (((k // INNER) % HALVES) ^ parity) + core) * peers + k for k in range(peers)
            ])
    return groups


def local(three_index, tile_mask, occ_density, virt_density):
    virt_count = three_index.shape[0]
    peers = lax.axis_size("aux")
    own = lax.axis_index("occ")
    my_half = (lax.axis_index("aux") // INNER) % HALVES
    by_half = virt_density.reshape(peers // (HALVES * INNER), HALVES, -1, virt_count)

    head = first_pack(tile_mask, three_index)
    ids = jnp.stack(lax.optimization_barrier((own, my_half, head))[:2]).astype(jnp.int32)
    others, *weights = rest_pack(tile_mask, ids, three_index, by_half, occ_density)
    virt, occ, table = (pltpu.with_memory_space_constraint(array, pltpu.HBM) for array in weights)
    mine = [head] + others

    chip_pairs = [(s, s ^ 2) for s in range(SLABS)]
    core_pairs = [(s, s ^ 1) for s in range(SLABS)]
    groups = exchange_groups(peers)
    done, acrosses, early = [], [], None
    last = len(mine) - 1
    besides = [lax.ppermute(part, "occ", core_pairs) for part in mine]
    for k, part in enumerate(mine):
        sent = part
        if k >= 2:
            sent, _ = lax.optimization_barrier((part, acrosses[k - 2]))
        across = lax.ppermute(sent, "occ", chip_pairs)
        beside = besides[k]
        partial = None
        if k in (0, last):
            own_part = part if k == 0 else lax.optimization_barrier((part, gamma))[0]
            partial = density(
                table, ids, (0, 2), (own_part, beside), virt, occ, ends=False, only=1 if k else None, into=early
            )
        before = (mine[1], partial) if k == 0 else (gamma, partial) if k == last else (gamma,)
        across, *before = lax.optimization_barrier((across,) + before)
        acrosses.append(across)
        diagonal = lax.ppermute(across, "occ", core_pairs)
        if partial is None:
            gamma = density(table, ids, (0, 1, 2, 3), (part, across, beside, diagonal), virt, occ)
        else:
            gamma = density(table, ids, (1, 3), (across, diagonal), virt, occ, partial=before[1])
        if k == 0:
            own_part, _ = lax.optimization_barrier((mine[last], gamma))
            beside = lax.ppermute(mine[last], "occ", core_pairs)
            early = density(table, ids, (0, 2), (own_part, beside), virt, occ, ends=False, only=0)
            gamma, early = lax.optimization_barrier((gamma, early))
        done.append(lax.all_to_all(
            gamma.reshape(virt_count, OCC, -1), ("occ", "aux"),
            split_axis=0, concat_axis=0, axis_index_groups=groups, tiled=True,
        ))
    return place_last(done[-1], assemble(done[:-1], peers, three_index.shape[2]))


def solution(mesh):
    return jax.shard_map(
        local,
        mesh=mesh,
        in_specs=(P(None, "occ", "aux"), P(), P(), P()),
        out_specs=P("aux", "occ", None),
        check_vma=False,
    )
```

```python
import functools

import jax
import jax.numpy as jnp
from jax import lax
from jax.experimental import pallas as pl
from jax.experimental.pallas import tpu as pltpu
from jax.sharding import PartitionSpec as P

VT = 6
CAP = 4
OCC = 8
SLABS = 4
FLIPS = (0, 2, 1, 3)
LANES = 128
GROUP = 32
ROWS = GROUP * OCC
FINE = 16
FROWS = FINE * OCC
HALVES = 2
SPAN = 96
INNER = 4
VMEM = 60 << 20


def iota(shape, dim):
    return lax.broadcasted_iota(jnp.int32, shape, dim)


def one_hot(condition):
    return jnp.where(condition, 1.0, 0.0).astype(jnp.bfloat16)


def dot(left, right):
    return jnp.dot(left, right, preferred_element_type=jnp.float32)


def permutation(back):
    shape = (ROWS, ROWS)
    fine, coarse = (iota(shape, 1), iota(shape, 0)) if back else (iota(shape, 0), iota(shape, 1))
    return one_hot((fine % GROUP == coarse // OCC) & (fine // GROUP == coarse % OCC))


def tile_of(mask_ref, slab, q):
    seen, tile = 0, 0
    for t in range(VT):
        seen = seen + mask_ref[slab, t]
        tile = tile + (seen <= q).astype(jnp.int32)
    return jnp.minimum(tile, VT - 1)


def transpose_rows(perm, columns):
    y = dot(perm, jnp.concatenate(columns, axis=1)).astype(jnp.bfloat16)
    return y[:, :LANES], y[:, LANES:]


def pack_rows(perm, x_ref, outs, first):
    for g in range(0, x_ref.shape[0] // GROUP, 2):
        for c, out in enumerate(outs):
            cols = slice((first + c) * LANES, (first + c + 1) * LANES)
            pair = transpose_rows(perm, [
                x_ref[n * GROUP:(n + 1) * GROUP, :, cols].reshape(ROWS, LANES) for n in (g, g + 1)
            ])
            for n in range(2):
                at = (g + n) * GROUP
                out[:, at:at + GROUP, :] = pair[n].reshape(OCC, GROUP, LANES)


def first_body(mask_ref, x_ref, out, tiles, packed, in_sems, out_sems):
    tile = tiles.shape[1]
    own = lax.axis_index("occ")
    arrivals, departures = [], []
    for q in range(CAP):
        at = pl.multiple_of(tile_of(mask_ref, own, q) * tile, tile)
        copy = pltpu.make_async_copy(x_ref.at[pl.ds(at, tile), :, pl.ds(0, LANES)], tiles.at[q], in_sems.at[q])
        copy.start()
        arrivals.append(copy)
    perm = permutation(False)
    for q in range(CAP):
        arrivals[q].wait()
        pack_rows(perm, tiles.at[q], [packed.at[q]], 0)
        copy = pltpu.make_async_copy(packed.at[q], out.at[:, pl.ds(q * tile, tile), :], out_sems.at[q])
        copy.start()
        departures.append(copy)
    for copy in departures:
        copy.wait()


def first_pack(mask, three_index):
    tile = three_index.shape[0] // VT
    return pl.pallas_call(
        first_body,
        out_shape=jax.ShapeDtypeStruct((OCC, CAP * tile, LANES), jnp.bfloat16),
        grid_spec=pltpu.PrefetchScalarGridSpec(
            num_scalar_prefetch=1,
            grid=(1,),
            in_specs=[pl.BlockSpec(memory_space=pl.ANY)],
            out_specs=pl.BlockSpec(memory_space=pl.ANY),
            scratch_shapes=[
                pltpu.VMEM((CAP, tile, OCC, LANES), jnp.bfloat16),
                pltpu.VMEM((CAP, OCC, tile, LANES), jnp.bfloat16),
                pltpu.SemaphoreType.DMA((CAP,)),
                pltpu.SemaphoreType.DMA((CAP,)),
            ],
        ),
        compiler_params=pltpu.CompilerParams(vmem_limit_bytes=VMEM),
        cost_estimate=pl.CostEstimate(flops=1 << 29, bytes_accessed=2 << 20, transcendentals=0),
    )(mask, three_index)


def rest_body(mask_ref, ids_ref, x_ref, v0_ref, v1_ref, d_ref, virt_out, occ_out, table_out, *outs):
    q = pl.program_id(0)
    own = ids_ref[0]
    pack_rows(permutation(False), x_ref, outs, 1)
    for which, v_ref in enumerate((v0_ref, v1_ref)):
        count = 0
        for t in range(VT):
            count = count + mask_ref[own ^ FLIPS[which], t]
        part = v_ref[...].reshape(-1, x_ref.shape[0])
        virt_out[which] = jnp.where(q < count, part, jnp.zeros_like(part))

    @pl.when(q == 0)
    def _():
        tile = x_ref.shape[0]
        for s in range(SLABS):
            seen = 0
            for t in range(VT):
                here = mask_ref[own ^ FLIPS[s], t]
                table_out[s, t] = jnp.where(here > 0, seen * tile, -1)
                seen = seen + here
        width = SLABS * FROWS
        shape = (SLABS * OCC, width)
        col = iota(shape, 1)
        slab = col // FROWS
        source = own
        for s in range(1, SLABS):
            source = jnp.where(slab == s, own ^ FLIPS[s], source)
        pick_cols = one_hot(iota(shape, 0) == source * OCC + col % FROWS // FINE)
        spread = dot(d_ref[...], pick_cols).astype(jnp.bfloat16)
        shape = (FROWS, SLABS * OCC)
        full = (FROWS, width)
        same = iota(full, 0) % FINE == iota(full, 1) % FINE
        for which in range(2):
            pick_rows = one_hot(iota(shape, 1) == (own ^ FLIPS[which]) * OCC + iota(shape, 0) // FINE)
            occ_out[which] = jnp.where(same, dot(pick_rows, spread), 0.0).astype(jnp.bfloat16)


def rest_pack(mask, ids, three_index, by_half, occ_density):
    virt_count, _, cols = three_index.shape
    tile = virt_count // VT
    blocks, _, span, _ = by_half.shape
    half_rows = blocks * span
    count = cols // LANES - 1

    def half_block(which):
        def index(q, mask, ids):
            half = ids[1] if which == 0 else 1 - ids[1]
            return 0, half, 0, tile_of(mask, ids[0] ^ FLIPS[which], q)
        return pl.BlockSpec((blocks, 1, span, tile), index)

    virt, occ, table, *packs = pl.pallas_call(
        rest_body,
        out_shape=[
            jax.ShapeDtypeStruct((2, half_rows, CAP * tile), jnp.bfloat16),
            jax.ShapeDtypeStruct((2, FROWS, SLABS * FROWS), jnp.bfloat16),
            jax.ShapeDtypeStruct((SLABS, VT), jnp.int32),
        ] + [jax.ShapeDtypeStruct((OCC, CAP * tile, LANES), jnp.bfloat16)] * count,
        grid_spec=pltpu.PrefetchScalarGridSpec(
            num_scalar_prefetch=2,
            grid=(CAP,),
            in_specs=[
                pl.BlockSpec((tile, OCC, cols), lambda q, mask, ids: (tile_of(mask, ids[0], q), 0, 0)),
                half_block(0),
                half_block(1),
                pl.BlockSpec(occ_density.shape, lambda q, mask, ids: (0, 0)),
            ],
            out_specs=[
                pl.BlockSpec((2, half_rows, tile), lambda q, mask, ids: (0, 0, q)),
                pl.BlockSpec((2, FROWS, SLABS * FROWS), lambda q, mask, ids: (0, 0, 0)),
                pl.BlockSpec(memory_space=pltpu.SMEM),
            ] + [pl.BlockSpec((OCC, tile, LANES), lambda q, mask, ids: (0, q, 0))] * count,
        ),
        compiler_params=pltpu.CompilerParams(vmem_limit_bytes=VMEM),
        cost_estimate=pl.CostEstimate(flops=3 << 30, bytes_accessed=12 << 20, transcendentals=0),
    )(mask, ids, three_index, by_half, by_half, occ_density)
    return packs, virt, occ, table


def density_body(slabs, begins, ends, *refs):
    table_ref, ids_ref, *refs = refs
    count = len(slabs)
    sources, (virt_in, occ_in), refs = refs[:count], refs[count:count + 2], refs[count + 2:]
    partial = None if begins else refs.pop(0)
    out, packs, virt_ref, occ_ref, total, mixed, result, in_sems, out_sems = refs
    if not ends:
        total = out
    depth = sources[0].shape[1]
    half_rows = virt_in.shape[1]
    blocks = half_rows // SPAN
    tile = depth // CAP
    arrivals = [
        pltpu.make_async_copy(ref, packs.at[n, :, pl.ds(0, depth), :], in_sems.at[n])
        for n, ref in enumerate(sources)
    ]
    direct = [(n, slab) for n, slab in enumerate(slabs) if slab < 2]
    virt_copy = pltpu.make_async_copy(virt_in, virt_ref, in_sems.at[count])
    occ_copy = pltpu.make_async_copy(occ_in, occ_ref, in_sems.at[count + 1])
    arrivals[0].start()
    if direct:
        virt_copy.start()
    for copy in arrivals[1:]:
        copy.start()
    occ_copy.start()
    for n in range(count):
        packs[n, :, depth:depth + FINE, :] = jnp.zeros((OCC, FINE, LANES), jnp.bfloat16)
    perm = permutation(True) if ends else None
    if direct:
        virt_copy.wait()
    for n, slab in direct:
        arrivals[n].wait()
        for i in range(0, OCC, 2):
            both = jnp.concatenate([packs[n, i, :depth], packs[n, i + 1, :depth]], axis=1)
            y = dot(virt_ref[slab], both)
            for j in range(2):
                part = y[:, j * LANES:(j + 1) * LANES]
                total[slab, i + j] = part if begins else part + partial[slab, i + j]
    for n, slab in enumerate(slabs):
        if slab >= 2:
            arrivals[n].wait()
    occ_copy.wait()
    departures = []
    for which in range(2):
        half = ids_ref[1] if which == 0 else 1 - ids_ref[1]
        base = total if which in slabs else partial
        weights = jnp.concatenate([occ_ref[which][:, s * FROWS:(s + 1) * FROWS] for s in slabs], axis=1)
        for first in range(0, half_rows, 2 * FINE):
            columns = []
            for row in (first, first + FINE):
                start = row // SPAN * (HALVES * SPAN) + row % SPAN + half * SPAN
                parts = []
                for n, s in enumerate(slabs):
                    at = table_ref[s, start // tile]
                    at = pl.multiple_of(jnp.where(at < 0, depth, at + start % tile), FINE)
                    parts.append(packs[n, :, pl.ds(at, FINE), :].reshape(FROWS, LANES))
                columns.append(jnp.concatenate(parts, axis=0))
            y = dot(weights, jnp.concatenate(columns, axis=1))
            for n in range(2):
                row = first + n * FINE
                part = y[:, n * LANES:(n + 1) * LANES].reshape(OCC, FINE, LANES)
                if base is not None:
                    part = part + base[which, :, row:row + FINE, :]
                if ends:
                    mixed[which, :, row:row + FINE, :] = part.astype(jnp.bfloat16)
                else:
                    total[which, :, row:row + FINE, :] = part
        if not ends:
            continue
        for first in range(0, half_rows, 2 * GROUP):
            pair = transpose_rows(perm, [
                mixed[which, :, row:row + GROUP, :].reshape(ROWS, LANES) for row in (first, first + GROUP)
            ])
            for n in range(2):
                at = (first + n * GROUP) * OCC
                result[which, at:at + ROWS, :] = pair[n]
        for b in range(blocks):
            start = pl.multiple_of((b * HALVES + half) * SPAN * OCC, SPAN * OCC)
            copy = pltpu.make_async_copy(
                result.at[which, pl.ds(b * SPAN * OCC, SPAN * OCC), :],
                out.at[pl.ds(start, SPAN * OCC), :],
                out_sems.at[which * blocks + b],
            )
            copy.start()
            departures.append(copy)
    for copy in departures:
        copy.wait()


def density(table, ids, slabs, packs, virt, occ, partial=None, ends=True):
    depth = packs[0].shape[1]
    half_rows = virt.shape[1]
    rows = 2 * half_rows * OCC
    sums = (2, OCC, half_rows, LANES)
    begins = partial is None
    share = len(slabs) * LANES
    extra = [] if begins else [partial]
    held = pl.BlockSpec(memory_space=pltpu.VMEM)
    unused = (OCC, LANES)
    return pl.pallas_call(
        functools.partial(density_body, slabs, begins, ends),
        out_shape=jax.ShapeDtypeStruct((rows, LANES), jnp.bfloat16) if ends else jax.ShapeDtypeStruct(sums, jnp.float32),
        grid_spec=pltpu.PrefetchScalarGridSpec(
            num_scalar_prefetch=2,
            grid=(1,),
            in_specs=[pl.BlockSpec(memory_space=pl.ANY)] * (len(slabs) + 2) + [held] * len(extra),
            out_specs=pl.BlockSpec(memory_space=pl.ANY) if ends else held,
            scratch_shapes=[
                pltpu.VMEM((len(slabs), OCC, depth + FINE, LANES), jnp.bfloat16),
                pltpu.VMEM(virt.shape if min(slabs) < 2 else unused, jnp.bfloat16),
                pltpu.VMEM(occ.shape, jnp.bfloat16),
                pltpu.VMEM(sums if ends and min(slabs) < 2 else unused, jnp.float32),
                pltpu.VMEM(sums if ends else unused, jnp.bfloat16),
                pltpu.VMEM((2, half_rows * OCC, LANES) if ends else unused, jnp.bfloat16),
                pltpu.SemaphoreType.DMA((len(slabs) + 2,)),
                pltpu.SemaphoreType.DMA((2 * half_rows // SPAN,)),
            ],
        ),
        compiler_params=pltpu.CompilerParams(vmem_limit_bytes=24 << 20),
        cost_estimate=pl.CostEstimate(
            flops=share * (rows * depth // 2 + 2 * rows * ROWS),
            bytes_accessed=share * OCC * depth * 2 + rows * LANES * 2,
            transcendentals=0,
        ),
    )(table, ids, *packs, virt, occ, *extra)


def assemble_body(*refs):
    count = len(refs) - 5
    ins, out = refs[:count], refs[count]
    arrived, whole, in_sems, out_sems = refs[count + 1:]
    rows = out.shape[0]
    peers = ins[0].shape[0] // rows
    cols = out.shape[2] // peers
    steps = peers // INNER

    def arrivals(n):
        part = pl.ds(pl.multiple_of(n * INNER * rows, INNER * rows), INNER * rows)
        return [
            pltpu.make_async_copy(ref.at[part], arrived.at[k, part], in_sems.at[n, k]) for k, ref in enumerate(ins)
        ]

    def departure(n):
        part = pl.ds(pl.multiple_of(n * INNER * cols, INNER * cols), INNER * cols)
        return pltpu.make_async_copy(whole.at[:, :, part], out.at[:, :, part], out_sems.at[n])

    def fetch(n, carry):
        for copy in arrivals(n):
            copy.start()
        return carry

    def place(n, carry):
        for copy in arrivals(n):
            copy.wait()
        for m in range(INNER):
            at = pl.multiple_of((n * INNER + m) * rows, rows)
            for k in range(count):
                first = pl.multiple_of((n * INNER + m) * cols + k * LANES, LANES)
                whole[:, :, pl.ds(first, LANES)] = arrived[k, pl.ds(at, rows)]
        departure(n).start()
        return carry

    def leave(n, carry):
        departure(n).wait()
        return carry

    lax.fori_loop(0, steps, fetch, 0)
    lax.fori_loop(0, steps, place, 0)
    lax.fori_loop(0, steps, leave, 0)


def assemble(parts, peers, cols):
    rows = parts[0].shape[0] // peers
    shape = (rows, OCC, peers * cols)
    return pl.pallas_call(
        assemble_body,
        out_shape=jax.ShapeDtypeStruct(shape, jnp.bfloat16),
        in_specs=[pl.BlockSpec(memory_space=pl.ANY)] * len(parts),
        out_specs=pl.BlockSpec(memory_space=pl.ANY),
        scratch_shapes=[
            pltpu.VMEM((len(parts),) + parts[0].shape, jnp.bfloat16),
            pltpu.VMEM(shape, jnp.bfloat16),
            pltpu.SemaphoreType.DMA((peers // INNER, len(parts))),
            pltpu.SemaphoreType.DMA((peers // INNER,)),
        ],
        compiler_params=pltpu.CompilerParams(vmem_limit_bytes=VMEM),
        cost_estimate=pl.CostEstimate(
            flops=0, bytes_accessed=4 * rows * OCC * shape[2], transcendentals=0
        ),
    )(*parts)


def place_body(part, _, out, sems):
    rows = out.shape[0]
    peers = part.shape[0] // rows
    cols = out.shape[2] // peers
    copies = []
    for m in range(peers):
        copy = pltpu.make_async_copy(
            part.at[pl.ds(m * rows, rows)],
            out.at[:, :, pl.ds((m + 1) * cols - LANES, LANES)],
            sems.at[m],
        )
        copy.start()
        copies.append(copy)
    for copy in copies:
        copy.wait()


def place_last(part, whole):
    peers = part.shape[0] // whole.shape[0]
    return pl.pallas_call(
        place_body,
        out_shape=jax.ShapeDtypeStruct(whole.shape, whole.dtype),
        in_specs=[pl.BlockSpec(memory_space=pltpu.VMEM), pl.BlockSpec(memory_space=pl.ANY)],
        out_specs=pl.BlockSpec(memory_space=pl.ANY),
        scratch_shapes=[pltpu.SemaphoreType.DMA((peers,))],
        input_output_aliases={1: 0},
        compiler_params=pltpu.CompilerParams(vmem_limit_bytes=8 << 20),
        cost_estimate=pl.CostEstimate(flops=0, bytes_accessed=4 * part.size, transcendentals=0),
    )(part, whole)


def exchange_groups(peers):
    groups = []
    for parity in range(2):
        for core in range(2):
            groups.append([
                (2 * (((k // INNER) % HALVES) ^ parity) + core) * peers + k for k in range(peers)
            ])
    return groups


def local(three_index, tile_mask, occ_density, virt_density):
    virt_count = three_index.shape[0]
    peers = lax.axis_size("aux")
    own = lax.axis_index("occ")
    my_half = (lax.axis_index("aux") // INNER) % HALVES
    by_half = virt_density.reshape(peers // (HALVES * INNER), HALVES, -1, virt_count)

    head = first_pack(tile_mask, three_index)
    ids = jnp.stack(lax.optimization_barrier((own, my_half, head))[:2]).astype(jnp.int32)
    others, *weights = rest_pack(tile_mask, ids, three_index, by_half, occ_density)
    virt, occ, table = (pltpu.with_memory_space_constraint(array, pltpu.HBM) for array in weights)
    mine = [head] + others

    chip_pairs = [(s, s ^ 2) for s in range(SLABS)]
    core_pairs = [(s, s ^ 1) for s in range(SLABS)]
    groups = exchange_groups(peers)
    done, acrosses = [], []
    last = len(mine) - 1
    besides = [lax.ppermute(part, "occ", core_pairs) for part in mine]
    for k, part in enumerate(mine):
        sent = part
        if k >= 2:
            sent, _ = lax.optimization_barrier((part, acrosses[k - 2]))
        across = lax.ppermute(sent, "occ", chip_pairs)
        beside = besides[k]
        partial = None
        if k in (0, last):
            own_part = part if k == 0 else lax.optimization_barrier((part, gamma))[0]
            partial = density(table, ids, (0, 2), (own_part, beside), virt, occ, ends=False)
        before = (mine[1], partial) if k == 0 else (gamma, partial) if k == last else (gamma,)
        across, *before = lax.optimization_barrier((across,) + before)
        acrosses.append(across)
        diagonal = lax.ppermute(across, "occ", core_pairs)
        if partial is None:
            gamma = density(table, ids, (0, 1, 2, 3), (part, across, beside, diagonal), virt, occ)
        else:
            partial = density(table, ids, (1,), (across,), virt, occ, partial=before[1], ends=False)
            gamma = density(table, ids, (3,), (diagonal,), virt, occ, partial=partial)
        done.append(lax.all_to_all(
            gamma.reshape(virt_count, OCC, -1), ("occ", "aux"),
            split_axis=0, concat_axis=0, axis_index_groups=groups, tiled=True,
        ))
    return place_last(done[-1], assemble(done[:-1], peers, three_index.shape[2]))


def solution(mesh):
    return jax.shard_map(
        local,
        mesh=mesh,
        in_specs=(P(None, "occ", "aux"), P(), P(), P()),
        out_specs=P("aux", "occ", None),
        check_vma=False,
    )
```

```python
import functools

import jax
import jax.numpy as jnp
from jax import lax
from jax.experimental import pallas as pl
from jax.experimental.pallas import tpu as pltpu
from jax.sharding import PartitionSpec as P

VT = 6
CAP = 4
OCC = 8
SLABS = 4
FLIPS = (0, 2, 1, 3)
LANES = 128
GROUP = 32
ROWS = GROUP * OCC
FINE = 16
FROWS = FINE * OCC
HALVES = 2
SPAN = 96
INNER = 4
VMEM = 60 << 20


def iota(shape, dim):
    return lax.broadcasted_iota(jnp.int32, shape, dim)


def one_hot(condition):
    return jnp.where(condition, 1.0, 0.0).astype(jnp.bfloat16)


def dot(left, right):
    return jnp.dot(left, right, preferred_element_type=jnp.float32)


def permutation(back):
    shape = (ROWS, ROWS)
    fine, coarse = (iota(shape, 1), iota(shape, 0)) if back else (iota(shape, 0), iota(shape, 1))
    return one_hot((fine % GROUP == coarse // OCC) & (fine // GROUP == coarse % OCC))


def tile_of(mask_ref, slab, q):
    seen, tile = 0, 0
    for t in range(VT):
        seen = seen + mask_ref[slab, t]
        tile = tile + (seen <= q).astype(jnp.int32)
    return jnp.minimum(tile, VT - 1)


def transpose_rows(perm, columns):
    y = dot(perm, jnp.concatenate(columns, axis=1)).astype(jnp.bfloat16)
    return y[:, :LANES], y[:, LANES:]


def pack_rows(perm, x_ref, outs, first):
    for g in range(0, x_ref.shape[0] // GROUP, 2):
        for c, out in enumerate(outs):
            cols = slice((first + c) * LANES, (first + c + 1) * LANES)
            pair = transpose_rows(perm, [
                x_ref[n * GROUP:(n + 1) * GROUP, :, cols].reshape(ROWS, LANES) for n in (g, g + 1)
            ])
            for n in range(2):
                at = (g + n) * GROUP
                out[:, at:at + GROUP, :] = pair[n].reshape(OCC, GROUP, LANES)


def first_body(mask_ref, x_ref, out, tiles, packed, in_sems, out_sems):
    tile = tiles.shape[1]
    own = lax.axis_index("occ")
    arrivals, departures = [], []
    for q in range(CAP):
        at = pl.multiple_of(tile_of(mask_ref, own, q) * tile, tile)
        copy = pltpu.make_async_copy(x_ref.at[pl.ds(at, tile), :, pl.ds(0, LANES)], tiles.at[q], in_sems.at[q])
        copy.start()
        arrivals.append(copy)
    perm = permutation(False)
    for q in range(CAP):
        arrivals[q].wait()
        pack_rows(perm, tiles.at[q], [packed.at[q]], 0)
        copy = pltpu.make_async_copy(packed.at[q], out.at[:, pl.ds(q * tile, tile), :], out_sems.at[q])
        copy.start()
        departures.append(copy)
    for copy in departures:
        copy.wait()


def first_pack(mask, three_index):
    tile = three_index.shape[0] // VT
    return pl.pallas_call(
        first_body,
        out_shape=jax.ShapeDtypeStruct((OCC, CAP * tile, LANES), jnp.bfloat16),
        grid_spec=pltpu.PrefetchScalarGridSpec(
            num_scalar_prefetch=1,
            grid=(1,),
            in_specs=[pl.BlockSpec(memory_space=pl.ANY)],
            out_specs=pl.BlockSpec(memory_space=pl.ANY),
            scratch_shapes=[
                pltpu.VMEM((CAP, tile, OCC, LANES), jnp.bfloat16),
                pltpu.VMEM((CAP, OCC, tile, LANES), jnp.bfloat16),
                pltpu.SemaphoreType.DMA((CAP,)),
                pltpu.SemaphoreType.DMA((CAP,)),
            ],
        ),
        compiler_params=pltpu.CompilerParams(vmem_limit_bytes=VMEM),
        cost_estimate=pl.CostEstimate(flops=1 << 29, bytes_accessed=2 << 20, transcendentals=0),
    )(mask, three_index)


def rest_body(mask_ref, ids_ref, x_ref, v0_ref, v1_ref, d_ref, virt_out, occ_out, table_out, *outs):
    q = pl.program_id(0)
    own = ids_ref[0]
    pack_rows(permutation(False), x_ref, outs, 1)
    for which, v_ref in enumerate((v0_ref, v1_ref)):
        count = 0
        for t in range(VT):
            count = count + mask_ref[own ^ FLIPS[which], t]
        part = v_ref[...].reshape(-1, x_ref.shape[0])
        virt_out[which] = jnp.where(q < count, part, jnp.zeros_like(part))

    @pl.when(q == 0)
    def _():
        tile = x_ref.shape[0]
        for s in range(SLABS):
            seen = 0
            for t in range(VT):
                here = mask_ref[own ^ FLIPS[s], t]
                table_out[s, t] = jnp.where(here > 0, seen * tile, -1)
                seen = seen + here
        width = SLABS * FROWS
        shape = (SLABS * OCC, width)
        col = iota(shape, 1)
        slab = col // FROWS
        source = own
        for s in range(1, SLABS):
            source = jnp.where(slab == s, own ^ FLIPS[s], source)
        pick_cols = one_hot(iota(shape, 0) == source * OCC + col % FROWS // FINE)
        spread = dot(d_ref[...], pick_cols).astype(jnp.bfloat16)
        shape = (FROWS, SLABS * OCC)
        full = (FROWS, width)
        same = iota(full, 0) % FINE == iota(full, 1) % FINE
        for which in range(2):
            pick_rows = one_hot(iota(shape, 1) == (own ^ FLIPS[which]) * OCC + iota(shape, 0) // FINE)
            occ_out[which] = jnp.where(same, dot(pick_rows, spread), 0.0).astype(jnp.bfloat16)


def rest_pack(mask, ids, three_index, by_half, occ_density):
    virt_count, _, cols = three_index.shape
    tile = virt_count // VT
    blocks, _, span, _ = by_half.shape
    half_rows = blocks * span
    count = cols // LANES - 1

    def half_block(which):
        def index(q, mask, ids):
            half = ids[1] if which == 0 else 1 - ids[1]
            return 0, half, 0, tile_of(mask, ids[0] ^ FLIPS[which], q)
        return pl.BlockSpec((blocks, 1, span, tile), index)

    virt, occ, table, *packs = pl.pallas_call(
        rest_body,
        out_shape=[
            jax.ShapeDtypeStruct((2, half_rows, CAP * tile), jnp.bfloat16),
            jax.ShapeDtypeStruct((2, FROWS, SLABS * FROWS), jnp.bfloat16),
            jax.ShapeDtypeStruct((SLABS, VT), jnp.int32),
        ] + [jax.ShapeDtypeStruct((OCC, CAP * tile, LANES), jnp.bfloat16)] * count,
        grid_spec=pltpu.PrefetchScalarGridSpec(
            num_scalar_prefetch=2,
            grid=(CAP,),
            in_specs=[
                pl.BlockSpec((tile, OCC, cols), lambda q, mask, ids: (tile_of(mask, ids[0], q), 0, 0)),
                half_block(0),
                half_block(1),
                pl.BlockSpec(occ_density.shape, lambda q, mask, ids: (0, 0)),
            ],
            out_specs=[
                pl.BlockSpec((2, half_rows, tile), lambda q, mask, ids: (0, 0, q)),
                pl.BlockSpec((2, FROWS, SLABS * FROWS), lambda q, mask, ids: (0, 0, 0)),
                pl.BlockSpec(memory_space=pltpu.SMEM),
            ] + [pl.BlockSpec((OCC, tile, LANES), lambda q, mask, ids: (0, q, 0))] * count,
        ),
        compiler_params=pltpu.CompilerParams(vmem_limit_bytes=VMEM),
        cost_estimate=pl.CostEstimate(flops=3 << 30, bytes_accessed=12 << 20, transcendentals=0),
    )(mask, ids, three_index, by_half, by_half, occ_density)
    return packs, virt, occ, table


def density_body(slabs, begins, ends, *refs):
    table_ref, ids_ref, *refs = refs
    count = len(slabs)
    sources, (virt_in, occ_in), refs = refs[:count], refs[count:count + 2], refs[count + 2:]
    if not begins:
        partial, *refs = refs
    out, packs, virt_ref, occ_ref, total, mixed, result, in_sems, out_sems = refs
    depth = sources[0].shape[1]
    half_rows = virt_ref.shape[1]
    blocks = half_rows // SPAN
    tile = depth // CAP
    targets = [packs.at[n, :, pl.ds(0, depth), :] for n in range(count)] + [virt_ref, occ_ref]
    arrivals = [
        pltpu.make_async_copy(ref, target, in_sems.at[n])
        for n, (ref, target) in enumerate(zip(list(sources) + [virt_in, occ_in], targets))
    ]
    if not begins:
        arrivals.append(pltpu.make_async_copy(partial, total, in_sems.at[count + 2]))
    for n in [0, count] + list(range(1, count)) + list(range(count + 1, len(arrivals))):
        arrivals[n].start()
    for n in range(count):
        packs[n, :, depth:depth + FINE, :] = jnp.zeros((OCC, FINE, LANES), jnp.bfloat16)
    perm = permutation(True) if ends else None
    waited = set()

    def arrived(n):
        if n not in waited:
            waited.add(n)
            arrivals[n].wait()

    arrived(count)
    if not begins:
        arrived(count + 2)
    for n, slab in enumerate(slabs):
        if slab >= 2:
            continue
        arrived(n)
        for i in range(0, OCC, 2):
            both = jnp.concatenate([packs[n, i, :depth], packs[n, i + 1, :depth]], axis=1)
            y = dot(virt_ref[slab], both)
            for j in range(2):
                part = y[:, j * LANES:(j + 1) * LANES]
                total[slab, i + j] = part if begins else part + total[slab, i + j]
    for n in range(len(arrivals)):
        arrived(n)
    fresh = [which for which in range(2) if begins and which not in slabs]
    departures = []
    for which in range(2):
        half = ids_ref[1] if which == 0 else 1 - ids_ref[1]
        weights = jnp.concatenate([occ_ref[which][:, s * FROWS:(s + 1) * FROWS] for s in slabs], axis=1)
        for first in range(0, half_rows, 2 * FINE):
            columns = []
            for row in (first, first + FINE):
                start = row // SPAN * (HALVES * SPAN) + row % SPAN + half * SPAN
                parts = []
                for n, s in enumerate(slabs):
                    base = table_ref[s, start // tile]
                    at = pl.multiple_of(jnp.where(base < 0, depth, base + start % tile), FINE)
                    parts.append(packs[n, :, pl.ds(at, FINE), :].reshape(FROWS, LANES))
                columns.append(jnp.concatenate(parts, axis=0))
            y = dot(weights, jnp.concatenate(columns, axis=1))
            for n in range(2):
                row = first + n * FINE
                part = y[:, n * LANES:(n + 1) * LANES].reshape(OCC, FINE, LANES)
                if which not in fresh:
                    part = part + total[which, :, row:row + FINE, :]
                if ends:
                    mixed[which, :, row:row + FINE, :] = part.astype(jnp.bfloat16)
                else:
                    total[which, :, row:row + FINE, :] = part
        if not ends:
            copy = pltpu.make_async_copy(total.at[which], out.at[which], out_sems.at[which])
            copy.start()
            departures.append(copy)
            continue
        for first in range(0, half_rows, 2 * GROUP):
            pair = transpose_rows(perm, [
                mixed[which, :, row:row + GROUP, :].reshape(ROWS, LANES) for row in (first, first + GROUP)
            ])
            for n in range(2):
                at = (first + n * GROUP) * OCC
                result[which, at:at + ROWS, :] = pair[n]
        for b in range(blocks):
            start = pl.multiple_of((b * HALVES + half) * SPAN * OCC, SPAN * OCC)
            copy = pltpu.make_async_copy(
                result.at[which, pl.ds(b * SPAN * OCC, SPAN * OCC), :],
                out.at[pl.ds(start, SPAN * OCC), :],
                out_sems.at[which * blocks + b],
            )
            copy.start()
            departures.append(copy)
    for copy in departures:
        copy.wait()


def density(table, ids, slabs, packs, virt, occ, partial=None, ends=True):
    depth = packs[0].shape[1]
    half_rows = virt.shape[1]
    rows = 2 * half_rows * OCC
    sums = (2, OCC, half_rows, LANES)
    begins = partial is None
    share = len(slabs) * LANES
    extra = [] if begins else [partial]
    return pl.pallas_call(
        functools.partial(density_body, slabs, begins, ends),
        out_shape=jax.ShapeDtypeStruct((rows, LANES), jnp.bfloat16) if ends else jax.ShapeDtypeStruct(sums, jnp.float32),
        grid_spec=pltpu.PrefetchScalarGridSpec(
            num_scalar_prefetch=2,
            grid=(1,),
            in_specs=[pl.BlockSpec(memory_space=pl.ANY)] * (len(slabs) + 2 + len(extra)),
            out_specs=pl.BlockSpec(memory_space=pl.ANY),
            scratch_shapes=[
                pltpu.VMEM((len(slabs), OCC, depth + FINE, LANES), jnp.bfloat16),
                pltpu.VMEM(virt.shape, jnp.bfloat16),
                pltpu.VMEM(occ.shape, jnp.bfloat16),
                pltpu.VMEM(sums, jnp.float32),
                pltpu.VMEM(sums if ends else (OCC, LANES), jnp.bfloat16),
                pltpu.VMEM((2, half_rows * OCC, LANES) if ends else (OCC, LANES), jnp.bfloat16),
                pltpu.SemaphoreType.DMA((len(slabs) + 3,)),
                pltpu.SemaphoreType.DMA((2 * half_rows // SPAN,)),
            ],
        ),
        compiler_params=pltpu.CompilerParams(vmem_limit_bytes=24 << 20),
        cost_estimate=pl.CostEstimate(
            flops=share * (rows * depth // 2 + 2 * rows * ROWS),
            bytes_accessed=share * OCC * depth * 2 + rows * LANES * 2,
            transcendentals=0,
        ),
    )(table, ids, *packs, virt, occ, *extra)


def assemble_body(*refs):
    count = len(refs) - 5
    ins, out = refs[:count], refs[count]
    arrived, whole, in_sems, out_sems = refs[count + 1:]
    rows = out.shape[0]
    peers = ins[0].shape[0] // rows
    cols = out.shape[2] // peers
    steps = peers // INNER

    def arrivals(n):
        part = pl.ds(pl.multiple_of(n * INNER * rows, INNER * rows), INNER * rows)
        return [
            pltpu.make_async_copy(ref.at[part], arrived.at[k, part], in_sems.at[n, k]) for k, ref in enumerate(ins)
        ]

    def departure(n):
        part = pl.ds(pl.multiple_of(n * INNER * cols, INNER * cols), INNER * cols)
        return pltpu.make_async_copy(whole.at[:, :, part], out.at[:, :, part], out_sems.at[n])

    def fetch(n, carry):
        for copy in arrivals(n):
            copy.start()
        return carry

    def place(n, carry):
        for copy in arrivals(n):
            copy.wait()
        for m in range(INNER):
            at = pl.multiple_of((n * INNER + m) * rows, rows)
            for k in range(count):
                first = pl.multiple_of((n * INNER + m) * cols + k * LANES, LANES)
                whole[:, :, pl.ds(first, LANES)] = arrived[k, pl.ds(at, rows)]
        departure(n).start()
        return carry

    def leave(n, carry):
        departure(n).wait()
        return carry

    lax.fori_loop(0, steps, fetch, 0)
    lax.fori_loop(0, steps, place, 0)
    lax.fori_loop(0, steps, leave, 0)


def assemble(parts, peers, cols):
    rows = parts[0].shape[0] // peers
    shape = (rows, OCC, peers * cols)
    return pl.pallas_call(
        assemble_body,
        out_shape=jax.ShapeDtypeStruct(shape, jnp.bfloat16),
        in_specs=[pl.BlockSpec(memory_space=pl.ANY)] * len(parts),
        out_specs=pl.BlockSpec(memory_space=pl.ANY),
        scratch_shapes=[
            pltpu.VMEM((len(parts),) + parts[0].shape, jnp.bfloat16),
            pltpu.VMEM(shape, jnp.bfloat16),
            pltpu.SemaphoreType.DMA((peers // INNER, len(parts))),
            pltpu.SemaphoreType.DMA((peers // INNER,)),
        ],
        compiler_params=pltpu.CompilerParams(vmem_limit_bytes=VMEM),
        cost_estimate=pl.CostEstimate(
            flops=0, bytes_accessed=4 * rows * OCC * shape[2], transcendentals=0
        ),
    )(*parts)


def place_body(part, _, out, sems):
    rows = out.shape[0]
    peers = part.shape[0] // rows
    cols = out.shape[2] // peers
    copies = []
    for m in range(peers):
        copy = pltpu.make_async_copy(
            part.at[pl.ds(m * rows, rows)],
            out.at[:, :, pl.ds((m + 1) * cols - LANES, LANES)],
            sems.at[m],
        )
        copy.start()
        copies.append(copy)
    for copy in copies:
        copy.wait()


def place_last(part, whole):
    peers = part.shape[0] // whole.shape[0]
    return pl.pallas_call(
        place_body,
        out_shape=jax.ShapeDtypeStruct(whole.shape, whole.dtype),
        in_specs=[pl.BlockSpec(memory_space=pltpu.VMEM), pl.BlockSpec(memory_space=pl.ANY)],
        out_specs=pl.BlockSpec(memory_space=pl.ANY),
        scratch_shapes=[pltpu.SemaphoreType.DMA((peers,))],
        input_output_aliases={1: 0},
        compiler_params=pltpu.CompilerParams(vmem_limit_bytes=8 << 20),
        cost_estimate=pl.CostEstimate(flops=0, bytes_accessed=4 * part.size, transcendentals=0),
    )(part, whole)


def exchange_groups(peers):
    groups = []
    for parity in range(2):
        for core in range(2):
            groups.append([
                (2 * (((k // INNER) % HALVES) ^ parity) + core) * peers + k for k in range(peers)
            ])
    return groups


def local(three_index, tile_mask, occ_density, virt_density):
    virt_count = three_index.shape[0]
    peers = lax.axis_size("aux")
    own = lax.axis_index("occ")
    my_half = (lax.axis_index("aux") // INNER) % HALVES
    by_half = virt_density.reshape(peers // (HALVES * INNER), HALVES, -1, virt_count)

    head = first_pack(tile_mask, three_index)
    ids = jnp.stack(lax.optimization_barrier((own, my_half, head))[:2]).astype(jnp.int32)
    others, *weights = rest_pack(tile_mask, ids, three_index, by_half, occ_density)
    virt, occ, table = (pltpu.with_memory_space_constraint(array, pltpu.HBM) for array in weights)
    mine = [head] + others

    chip_pairs = [(s, s ^ 2) for s in range(SLABS)]
    core_pairs = [(s, s ^ 1) for s in range(SLABS)]
    groups = exchange_groups(peers)
    done = []
    arrivals = [lax.ppermute(part, "occ", chip_pairs) for part in mine]
    last = len(mine) - 1
    besides = [lax.ppermute(part, "occ", core_pairs) for part in mine]
    for k, part in enumerate(mine):
        across = arrivals[k]
        beside = besides[k]
        partial = None
        if k in (0, last):
            own_part = part if k == 0 else lax.optimization_barrier((part, gamma))[0]
            partial = density(table, ids, (0, 2), (own_part, beside), virt, occ, ends=False)
        before = (mine[1], partial) if k == 0 else (gamma, partial) if k == last else (gamma,)
        across, *before = lax.optimization_barrier((across,) + before)
        diagonal = lax.ppermute(across, "occ", core_pairs)
        if partial is None:
            gamma = density(table, ids, (0, 1, 2, 3), (part, across, beside, diagonal), virt, occ)
        else:
            gamma = density(table, ids, (1, 3), (across, diagonal), virt, occ, partial=before[1])
        done.append(lax.all_to_all(
            gamma.reshape(virt_count, OCC, -1), ("occ", "aux"),
            split_axis=0, concat_axis=0, axis_index_groups=groups, tiled=True,
        ))
    return place_last(done[-1], assemble(done[:-1], peers, three_index.shape[2]))


def solution(mesh):
    return jax.shard_map(
        local,
        mesh=mesh,
        in_specs=(P(None, "occ", "aux"), P(), P(), P()),
        out_specs=P("aux", "occ", None),
        check_vma=False,
    )
```

```python
import functools

import jax
import jax.numpy as jnp
from jax import lax
from jax.experimental import pallas as pl
from jax.experimental.pallas import tpu as pltpu
from jax.sharding import PartitionSpec as P

VT = 6
CAP = 4
OCC = 8
SLABS = 4
FLIPS = (0, 2, 1, 3)
LANES = 128
GROUP = 32
ROWS = GROUP * OCC
FINE = 16
FROWS = FINE * OCC
HALVES = 2
SPAN = 96
INNER = 4
VMEM = 60 << 20


def iota(shape, dim):
    return lax.broadcasted_iota(jnp.int32, shape, dim)


def one_hot(condition):
    return jnp.where(condition, 1.0, 0.0).astype(jnp.bfloat16)


def dot(left, right):
    return jnp.dot(left, right, preferred_element_type=jnp.float32)


def permutation(back):
    shape = (ROWS, ROWS)
    fine, coarse = (iota(shape, 1), iota(shape, 0)) if back else (iota(shape, 0), iota(shape, 1))
    return one_hot((fine % GROUP == coarse // OCC) & (fine // GROUP == coarse % OCC))


def tile_of(mask_ref, slab, q):
    seen, tile = 0, 0
    for t in range(VT):
        seen = seen + mask_ref[slab, t]
        tile = tile + (seen <= q).astype(jnp.int32)
    return jnp.minimum(tile, VT - 1)


def transpose_rows(perm, columns):
    y = dot(perm, jnp.concatenate(columns, axis=1)).astype(jnp.bfloat16)
    return y[:, :LANES], y[:, LANES:]


def pack_rows(perm, x_ref, outs, first):
    for g in range(0, x_ref.shape[0] // GROUP, 2):
        for c, out in enumerate(outs):
            cols = slice((first + c) * LANES, (first + c + 1) * LANES)
            pair = transpose_rows(perm, [
                x_ref[n * GROUP:(n + 1) * GROUP, :, cols].reshape(ROWS, LANES) for n in (g, g + 1)
            ])
            for n in range(2):
                at = (g + n) * GROUP
                out[:, at:at + GROUP, :] = pair[n].reshape(OCC, GROUP, LANES)


def first_body(mask_ref, x_ref, out, tiles, packed, in_sems, out_sems):
    tile = tiles.shape[1]
    own = lax.axis_index("occ")
    arrivals, departures = [], []
    for q in range(CAP):
        at = pl.multiple_of(tile_of(mask_ref, own, q) * tile, tile)
        copy = pltpu.make_async_copy(x_ref.at[pl.ds(at, tile), :, pl.ds(0, LANES)], tiles.at[q], in_sems.at[q])
        copy.start()
        arrivals.append(copy)
    perm = permutation(False)
    for q in range(CAP):
        arrivals[q].wait()
        pack_rows(perm, tiles.at[q], [packed.at[q]], 0)
        copy = pltpu.make_async_copy(packed.at[q], out.at[:, pl.ds(q * tile, tile), :], out_sems.at[q])
        copy.start()
        departures.append(copy)
    for copy in departures:
        copy.wait()


def first_pack(mask, three_index):
    tile = three_index.shape[0] // VT
    return pl.pallas_call(
        first_body,
        out_shape=jax.ShapeDtypeStruct((OCC, CAP * tile, LANES), jnp.bfloat16),
        grid_spec=pltpu.PrefetchScalarGridSpec(
            num_scalar_prefetch=1,
            grid=(1,),
            in_specs=[pl.BlockSpec(memory_space=pl.ANY)],
            out_specs=pl.BlockSpec(memory_space=pl.ANY),
            scratch_shapes=[
                pltpu.VMEM((CAP, tile, OCC, LANES), jnp.bfloat16),
                pltpu.VMEM((CAP, OCC, tile, LANES), jnp.bfloat16),
                pltpu.SemaphoreType.DMA((CAP,)),
                pltpu.SemaphoreType.DMA((CAP,)),
            ],
        ),
        compiler_params=pltpu.CompilerParams(vmem_limit_bytes=VMEM),
        cost_estimate=pl.CostEstimate(flops=1 << 29, bytes_accessed=2 << 20, transcendentals=0),
    )(mask, three_index)


def rest_body(mask_ref, ids_ref, x_ref, v0_ref, v1_ref, d_ref, virt_out, occ_out, table_out, *outs):
    q = pl.program_id(0)
    own = ids_ref[0]
    pack_rows(permutation(False), x_ref, outs, 1)
    for which, v_ref in enumerate((v0_ref, v1_ref)):
        count = 0
        for t in range(VT):
            count = count + mask_ref[own ^ FLIPS[which], t]
        part = v_ref[...].reshape(-1, x_ref.shape[0])
        virt_out[which] = jnp.where(q < count, part, jnp.zeros_like(part))

    @pl.when(q == 0)
    def _():
        tile = x_ref.shape[0]
        for s in range(SLABS):
            seen = 0
            for t in range(VT):
                here = mask_ref[own ^ FLIPS[s], t]
                table_out[s, t] = jnp.where(here > 0, seen * tile, -1)
                seen = seen + here
        width = SLABS * FROWS
        shape = (SLABS * OCC, width)
        col = iota(shape, 1)
        slab = col // FROWS
        source = own
        for s in range(1, SLABS):
            source = jnp.where(slab == s, own ^ FLIPS[s], source)
        pick_cols = one_hot(iota(shape, 0) == source * OCC + col % FROWS // FINE)
        spread = dot(d_ref[...], pick_cols).astype(jnp.bfloat16)
        shape = (FROWS, SLABS * OCC)
        full = (FROWS, width)
        same = iota(full, 0) % FINE == iota(full, 1) % FINE
        for which in range(2):
            pick_rows = one_hot(iota(shape, 1) == (own ^ FLIPS[which]) * OCC + iota(shape, 0) // FINE)
            occ_out[which] = jnp.where(same, dot(pick_rows, spread), 0.0).astype(jnp.bfloat16)


def rest_pack(mask, ids, three_index, by_half, occ_density):
    virt_count, _, cols = three_index.shape
    tile = virt_count // VT
    blocks, _, span, _ = by_half.shape
    half_rows = blocks * span
    count = cols // LANES - 1

    def half_block(which):
        def index(q, mask, ids):
            half = ids[1] if which == 0 else 1 - ids[1]
            return 0, half, 0, tile_of(mask, ids[0] ^ FLIPS[which], q)
        return pl.BlockSpec((blocks, 1, span, tile), index)

    virt, occ, table, *packs = pl.pallas_call(
        rest_body,
        out_shape=[
            jax.ShapeDtypeStruct((2, half_rows, CAP * tile), jnp.bfloat16),
            jax.ShapeDtypeStruct((2, FROWS, SLABS * FROWS), jnp.bfloat16),
            jax.ShapeDtypeStruct((SLABS, VT), jnp.int32),
        ] + [jax.ShapeDtypeStruct((OCC, CAP * tile, LANES), jnp.bfloat16)] * count,
        grid_spec=pltpu.PrefetchScalarGridSpec(
            num_scalar_prefetch=2,
            grid=(CAP,),
            in_specs=[
                pl.BlockSpec((tile, OCC, cols), lambda q, mask, ids: (tile_of(mask, ids[0], q), 0, 0)),
                half_block(0),
                half_block(1),
                pl.BlockSpec(occ_density.shape, lambda q, mask, ids: (0, 0)),
            ],
            out_specs=[
                pl.BlockSpec((2, half_rows, tile), lambda q, mask, ids: (0, 0, q)),
                pl.BlockSpec((2, FROWS, SLABS * FROWS), lambda q, mask, ids: (0, 0, 0)),
                pl.BlockSpec(memory_space=pltpu.SMEM),
            ] + [pl.BlockSpec((OCC, tile, LANES), lambda q, mask, ids: (0, q, 0))] * count,
        ),
        compiler_params=pltpu.CompilerParams(vmem_limit_bytes=VMEM),
        cost_estimate=pl.CostEstimate(flops=3 << 30, bytes_accessed=12 << 20, transcendentals=0),
    )(mask, ids, three_index, by_half, by_half, occ_density)
    return packs, virt, occ, table


def density_body(slabs, shape_of, begins, ends, *refs):
    table_ref, ids_ref, *refs = refs
    count = len(slabs)
    sources = [[refs.pop(0) for _ in range(pieces)] for pieces in shape_of]
    virt_in, occ_in, *refs = refs
    if not begins:
        partial, *refs = refs
    out, packs, virt_ref, occ_ref, total, mixed, result, in_sems, out_sems = refs
    depth = sources[0][0].shape[1]
    half_rows = virt_ref.shape[1]
    blocks = half_rows // SPAN
    tile = depth // CAP
    arrivals = []
    for n, parts in enumerate(sources):
        step = OCC // len(parts)
        arrivals.append([
            pltpu.make_async_copy(
                ref, packs.at[n, pl.ds(m * step, step), pl.ds(0, depth), :], in_sems.at[2 * n + m]
            )
            for m, ref in enumerate(parts)
        ])
    arrivals.append([pltpu.make_async_copy(virt_in, virt_ref, in_sems.at[2 * count])])
    arrivals.append([pltpu.make_async_copy(occ_in, occ_ref, in_sems.at[2 * count + 1])])
    if not begins:
        arrivals.append([pltpu.make_async_copy(partial, total, in_sems.at[2 * count + 2])])
    for n in [0, count] + list(range(1, count)) + list(range(count + 1, len(arrivals))):
        for copy in arrivals[n]:
            copy.start()
    for n in range(count):
        packs[n, :, depth:depth + FINE, :] = jnp.zeros((OCC, FINE, LANES), jnp.bfloat16)
    perm = permutation(True) if ends else None
    waited = set()

    def arrived(n):
        if n not in waited:
            waited.add(n)
            for copy in arrivals[n]:
                copy.wait()

    arrived(count)
    if not begins:
        arrived(count + 2)
    for n, slab in enumerate(slabs):
        if slab >= 2:
            continue
        arrived(n)
        for i in range(0, OCC, 2):
            both = jnp.concatenate([packs[n, i, :depth], packs[n, i + 1, :depth]], axis=1)
            y = dot(virt_ref[slab], both)
            for j in range(2):
                part = y[:, j * LANES:(j + 1) * LANES]
                total[slab, i + j] = part if begins else part + total[slab, i + j]
    for n in range(len(arrivals)):
        arrived(n)
    fresh = [which for which in range(2) if begins and which not in slabs]
    departures = []
    for which in range(2):
        half = ids_ref[1] if which == 0 else 1 - ids_ref[1]
        weights = jnp.concatenate([occ_ref[which][:, s * FROWS:(s + 1) * FROWS] for s in slabs], axis=1)
        for first in range(0, half_rows, 2 * FINE):
            columns = []
            for row in (first, first + FINE):
                start = row // SPAN * (HALVES * SPAN) + row % SPAN + half * SPAN
                parts = []
                for n, s in enumerate(slabs):
                    base = table_ref[s, start // tile]
                    at = pl.multiple_of(jnp.where(base < 0, depth, base + start % tile), FINE)
                    parts.append(packs[n, :, pl.ds(at, FINE), :].reshape(FROWS, LANES))
                columns.append(jnp.concatenate(parts, axis=0))
            y = dot(weights, jnp.concatenate(columns, axis=1))
            for n in range(2):
                row = first + n * FINE
                part = y[:, n * LANES:(n + 1) * LANES].reshape(OCC, FINE, LANES)
                if which not in fresh:
                    part = part + total[which, :, row:row + FINE, :]
                if ends:
                    mixed[which, :, row:row + FINE, :] = part.astype(jnp.bfloat16)
                else:
                    total[which, :, row:row + FINE, :] = part
        if not ends:
            copy = pltpu.make_async_copy(total.at[which], out.at[which], out_sems.at[which])
            copy.start()
            departures.append(copy)
            continue
        for first in range(0, half_rows, 2 * GROUP):
            pair = transpose_rows(perm, [
                mixed[which, :, row:row + GROUP, :].reshape(ROWS, LANES) for row in (first, first + GROUP)
            ])
            for n in range(2):
                at = (first + n * GROUP) * OCC
                result[which, at:at + ROWS, :] = pair[n]
        for b in range(blocks):
            start = pl.multiple_of((b * HALVES + half) * SPAN * OCC, SPAN * OCC)
            copy = pltpu.make_async_copy(
                result.at[which, pl.ds(b * SPAN * OCC, SPAN * OCC), :],
                out.at[pl.ds(start, SPAN * OCC), :],
                out_sems.at[which * blocks + b],
            )
            copy.start()
            departures.append(copy)
    for copy in departures:
        copy.wait()


def density(table, ids, slabs, packs, virt, occ, partial=None, ends=True):
    packs = [pack if isinstance(pack, list) else [pack] for pack in packs]
    shape_of = [len(pack) for pack in packs]
    depth = packs[0][0].shape[1]
    half_rows = virt.shape[1]
    rows = 2 * half_rows * OCC
    sums = (2, OCC, half_rows, LANES)
    begins = partial is None
    share = len(slabs) * LANES
    extra = [] if begins else [partial]
    return pl.pallas_call(
        functools.partial(density_body, slabs, shape_of, begins, ends),
        out_shape=jax.ShapeDtypeStruct((rows, LANES), jnp.bfloat16) if ends else jax.ShapeDtypeStruct(sums, jnp.float32),
        grid_spec=pltpu.PrefetchScalarGridSpec(
            num_scalar_prefetch=2,
            grid=(1,),
            in_specs=[pl.BlockSpec(memory_space=pl.ANY)] * (sum(shape_of) + 2 + len(extra)),
            out_specs=pl.BlockSpec(memory_space=pl.ANY),
            scratch_shapes=[
                pltpu.VMEM((len(slabs), OCC, depth + FINE, LANES), jnp.bfloat16),
                pltpu.VMEM(virt.shape, jnp.bfloat16),
                pltpu.VMEM(occ.shape, jnp.bfloat16),
                pltpu.VMEM(sums, jnp.float32),
                pltpu.VMEM(sums if ends else (OCC, LANES), jnp.bfloat16),
                pltpu.VMEM((2, half_rows * OCC, LANES) if ends else (OCC, LANES), jnp.bfloat16),
                pltpu.SemaphoreType.DMA((2 * len(slabs) + 3,)),
                pltpu.SemaphoreType.DMA((2 * half_rows // SPAN,)),
            ],
        ),
        compiler_params=pltpu.CompilerParams(vmem_limit_bytes=24 << 20),
        cost_estimate=pl.CostEstimate(
            flops=1 if ends else share * (rows * depth // 2 + 2 * rows * ROWS),
            bytes_accessed=1 if ends else share * OCC * depth * 2 + rows * LANES * 2,
            transcendentals=0,
        ),
    )(table, ids, *(piece for pack in packs for piece in pack), virt, occ, *extra)


def assemble_body(*refs):
    count = len(refs) - 5
    ins, out = refs[:count], refs[count]
    arrived, whole, in_sems, out_sems = refs[count + 1:]
    rows = out.shape[0]
    peers = ins[0].shape[0] // rows
    cols = out.shape[2] // peers
    steps = peers // INNER

    def arrivals(n):
        part = pl.ds(pl.multiple_of(n * INNER * rows, INNER * rows), INNER * rows)
        return [
            pltpu.make_async_copy(ref.at[part], arrived.at[k, part], in_sems.at[n, k]) for k, ref in enumerate(ins)
        ]

    def departure(n):
        part = pl.ds(pl.multiple_of(n * INNER * cols, INNER * cols), INNER * cols)
        return pltpu.make_async_copy(whole.at[:, :, part], out.at[:, :, part], out_sems.at[n])

    def fetch(n, carry):
        for copy in arrivals(n):
            copy.start()
        return carry

    def place(n, carry):
        for copy in arrivals(n):
            copy.wait()
        for m in range(INNER):
            at = pl.multiple_of((n * INNER + m) * rows, rows)
            for k in range(count):
                first = pl.multiple_of((n * INNER + m) * cols + k * LANES, LANES)
                whole[:, :, pl.ds(first, LANES)] = arrived[k, pl.ds(at, rows)]
        departure(n).start()
        return carry

    def leave(n, carry):
        departure(n).wait()
        return carry

    lax.fori_loop(0, steps, fetch, 0)
    lax.fori_loop(0, steps, place, 0)
    lax.fori_loop(0, steps, leave, 0)


def assemble(parts, peers, cols):
    rows = parts[0].shape[0] // peers
    shape = (rows, OCC, peers * cols)
    return pl.pallas_call(
        assemble_body,
        out_shape=jax.ShapeDtypeStruct(shape, jnp.bfloat16),
        in_specs=[pl.BlockSpec(memory_space=pl.ANY)] * len(parts),
        out_specs=pl.BlockSpec(memory_space=pl.ANY),
        scratch_shapes=[
            pltpu.VMEM((len(parts),) + parts[0].shape, jnp.bfloat16),
            pltpu.VMEM(shape, jnp.bfloat16),
            pltpu.SemaphoreType.DMA((peers // INNER, len(parts))),
            pltpu.SemaphoreType.DMA((peers // INNER,)),
        ],
        compiler_params=pltpu.CompilerParams(vmem_limit_bytes=VMEM),
        cost_estimate=pl.CostEstimate(
            flops=0, bytes_accessed=4 * rows * OCC * shape[2], transcendentals=0
        ),
    )(*parts)


def place_body(part, _, out, sems):
    rows = out.shape[0]
    peers = part.shape[0] // rows
    cols = out.shape[2] // peers
    copies = []
    for m in range(peers):
        copy = pltpu.make_async_copy(
            part.at[pl.ds(m * rows, rows)],
            out.at[:, :, pl.ds((m + 1) * cols - LANES, LANES)],
            sems.at[m],
        )
        copy.start()
        copies.append(copy)
    for copy in copies:
        copy.wait()


def place_last(part, whole):
    peers = part.shape[0] // whole.shape[0]
    return pl.pallas_call(
        place_body,
        out_shape=jax.ShapeDtypeStruct(whole.shape, whole.dtype),
        in_specs=[pl.BlockSpec(memory_space=pltpu.VMEM), pl.BlockSpec(memory_space=pl.ANY)],
        out_specs=pl.BlockSpec(memory_space=pl.ANY),
        scratch_shapes=[pltpu.SemaphoreType.DMA((peers,))],
        input_output_aliases={1: 0},
        compiler_params=pltpu.CompilerParams(vmem_limit_bytes=8 << 20),
        cost_estimate=pl.CostEstimate(flops=0, bytes_accessed=4 * part.size, transcendentals=0),
    )(part, whole)


def exchange_groups(peers):
    groups = []
    for parity in range(2):
        for core in range(2):
            groups.append([
                (2 * (((k // INNER) % HALVES) ^ parity) + core) * peers + k for k in range(peers)
            ])
    return groups


def local(three_index, tile_mask, occ_density, virt_density):
    virt_count = three_index.shape[0]
    peers = lax.axis_size("aux")
    own = lax.axis_index("occ")
    my_half = (lax.axis_index("aux") // INNER) % HALVES
    by_half = virt_density.reshape(peers // (HALVES * INNER), HALVES, -1, virt_count)

    head = first_pack(tile_mask, three_index)
    ids = jnp.stack(lax.optimization_barrier((own, my_half, head))[:2]).astype(jnp.int32)
    others, *weights = rest_pack(tile_mask, ids, three_index, by_half, occ_density)
    virt, occ, table = (pltpu.with_memory_space_constraint(array, pltpu.HBM) for array in weights)
    mine = [head] + others

    chip_pairs = [(s, s ^ 2) for s in range(SLABS)]
    core_pairs = [(s, s ^ 1) for s in range(SLABS)]
    groups = exchange_groups(peers)
    done = []
    arrivals = [lax.ppermute(part, "occ", chip_pairs) for part in mine]
    last = len(mine) - 1
    besides = [lax.ppermute(part, "occ", core_pairs) for part in mine]
    for k, part in enumerate(mine):
        across = arrivals[k]
        beside = besides[k]
        partial = None
        if k in (0, last):
            own_part = part if k == 0 else lax.optimization_barrier((part, gamma))[0]
            partial = density(table, ids, (0, 2), (own_part, beside), virt, occ, ends=False)
        before = (mine[1], partial) if k == 0 else (gamma, partial) if k == last else (gamma,)
        across, *before = lax.optimization_barrier((across,) + before)
        diagonal = [lax.ppermute(half, "occ", core_pairs) for half in jnp.split(across, 2, axis=0)]
        if partial is None:
            gamma = density(table, ids, (0, 1, 2, 3), (part, across, beside, diagonal), virt, occ)
        else:
            gamma = density(table, ids, (1, 3), (across, diagonal), virt, occ, partial=before[1])
        done.append(lax.all_to_all(
            gamma.reshape(virt_count, OCC, -1), ("occ", "aux"),
            split_axis=0, concat_axis=0, axis_index_groups=groups, tiled=True,
        ))
    return place_last(done[-1], assemble(done[:-1], peers, three_index.shape[2]))


def solution(mesh):
    return jax.shard_map(
        local,
        mesh=mesh,
        in_specs=(P(None, "occ", "aux"), P(), P(), P()),
        out_specs=P("aux", "occ", None),
        check_vma=False,
    )
```

```python
import functools

import jax
import jax.numpy as jnp
from jax import lax
from jax.experimental import pallas as pl
from jax.experimental.pallas import tpu as pltpu
from jax.sharding import PartitionSpec as P

VT = 6
CAP = 4
OCC = 8
SLABS = 4
FLIPS = (0, 2, 1, 3)
LANES = 128
GROUP = 32
ROWS = GROUP * OCC
FINE = 16
FROWS = FINE * OCC
HALVES = 2
SPAN = 96
INNER = 4
VMEM = 60 << 20


def block_of(place, core, blocks):
    return place + core * (blocks - 1 - 2 * place)


def iota(shape, dim):
    return lax.broadcasted_iota(jnp.int32, shape, dim)


def one_hot(condition):
    return jnp.where(condition, 1.0, 0.0).astype(jnp.bfloat16)


def dot(left, right):
    return jnp.dot(left, right, preferred_element_type=jnp.float32)


def permutation(back):
    shape = (ROWS, ROWS)
    fine, coarse = (iota(shape, 1), iota(shape, 0)) if back else (iota(shape, 0), iota(shape, 1))
    return one_hot((fine % GROUP == coarse // OCC) & (fine // GROUP == coarse % OCC))


def tile_of(mask_ref, slab, q):
    seen, tile = 0, 0
    for t in range(VT):
        seen = seen + mask_ref[slab, t]
        tile = tile + (seen <= q).astype(jnp.int32)
    return jnp.minimum(tile, VT - 1)


def transpose_rows(perm, columns):
    y = dot(perm, jnp.concatenate(columns, axis=1)).astype(jnp.bfloat16)
    return y[:, :LANES], y[:, LANES:]


def pack_rows(perm, x_ref, outs, first):
    for g in range(0, x_ref.shape[0] // GROUP, 2):
        for c, out in enumerate(outs):
            cols = slice((first + c) * LANES, (first + c + 1) * LANES)
            pair = transpose_rows(perm, [
                x_ref[n * GROUP:(n + 1) * GROUP, :, cols].reshape(ROWS, LANES) for n in (g, g + 1)
            ])
            for n in range(2):
                at = (g + n) * GROUP
                out[:, at:at + GROUP, :] = pair[n].reshape(OCC, GROUP, LANES)


def first_body(mask_ref, x_ref, out, tiles, packed, in_sems, out_sems):
    tile = tiles.shape[1]
    own = lax.axis_index("occ")
    arrivals, departures = [], []
    for q in range(CAP):
        at = pl.multiple_of(tile_of(mask_ref, own, q) * tile, tile)
        copy = pltpu.make_async_copy(x_ref.at[pl.ds(at, tile), :, pl.ds(0, LANES)], tiles.at[q], in_sems.at[q])
        copy.start()
        arrivals.append(copy)
    perm = permutation(False)
    for q in range(CAP):
        arrivals[q].wait()
        pack_rows(perm, tiles.at[q], [packed.at[q]], 0)
        copy = pltpu.make_async_copy(packed.at[q], out.at[:, pl.ds(q * tile, tile), :], out_sems.at[q])
        copy.start()
        departures.append(copy)
    for copy in departures:
        copy.wait()


def first_pack(mask, three_index):
    tile = three_index.shape[0] // VT
    return pl.pallas_call(
        first_body,
        out_shape=jax.ShapeDtypeStruct((OCC, CAP * tile, LANES), jnp.bfloat16),
        grid_spec=pltpu.PrefetchScalarGridSpec(
            num_scalar_prefetch=1,
            grid=(1,),
            in_specs=[pl.BlockSpec(memory_space=pl.ANY)],
            out_specs=pl.BlockSpec(memory_space=pl.ANY),
            scratch_shapes=[
                pltpu.VMEM((CAP, tile, OCC, LANES), jnp.bfloat16),
                pltpu.VMEM((CAP, OCC, tile, LANES), jnp.bfloat16),
                pltpu.SemaphoreType.DMA((CAP,)),
                pltpu.SemaphoreType.DMA((CAP,)),
            ],
        ),
        compiler_params=pltpu.CompilerParams(vmem_limit_bytes=VMEM),
        cost_estimate=pl.CostEstimate(flops=1 << 29, bytes_accessed=2 << 20, transcendentals=0),
    )(mask, three_index)


def rest_body(mask_ref, ids_ref, x_ref, v0_ref, v1_ref, d_ref, virt_out, occ_out, table_out, *outs):
    q = pl.program_id(0)
    own = ids_ref[0]
    pack_rows(permutation(False), x_ref, outs, 1)
    for which, v_ref in enumerate((v0_ref, v1_ref)):
        count = 0
        for t in range(VT):
            count = count + mask_ref[own ^ FLIPS[which], t]
        part = v_ref[...].reshape(-1, x_ref.shape[0])
        virt_out[which] = jnp.where(q < count, part, jnp.zeros_like(part))

    @pl.when(q == 0)
    def _():
        tile = x_ref.shape[0]
        for s in range(SLABS):
            seen = 0
            for t in range(VT):
                here = mask_ref[own ^ FLIPS[s], t]
                table_out[s, t] = jnp.where(here > 0, seen * tile, -1)
                seen = seen + here
        width = SLABS * FROWS
        shape = (SLABS * OCC, width)
        col = iota(shape, 1)
        slab = col // FROWS
        source = own
        for s in range(1, SLABS):
            source = jnp.where(slab == s, own ^ FLIPS[s], source)
        pick_cols = one_hot(iota(shape, 0) == source * OCC + col % FROWS // FINE)
        spread = dot(d_ref[...], pick_cols).astype(jnp.bfloat16)
        shape = (FROWS, SLABS * OCC)
        full = (FROWS, width)
        same = iota(full, 0) % FINE == iota(full, 1) % FINE
        for which in range(2):
            pick_rows = one_hot(iota(shape, 1) == (own ^ FLIPS[which]) * OCC + iota(shape, 0) // FINE)
            occ_out[which] = jnp.where(same, dot(pick_rows, spread), 0.0).astype(jnp.bfloat16)


def rest_pack(mask, ids, three_index, by_half, occ_density):
    virt_count, _, cols = three_index.shape
    tile = virt_count // VT
    blocks, _, span, _ = by_half.shape
    half_rows = blocks * span
    count = cols // LANES - 1

    def half_block(which):
        def index(q, mask, ids):
            half = ids[1] if which == 0 else 1 - ids[1]
            return 0, half, 0, tile_of(mask, ids[0] ^ FLIPS[which], q)
        return pl.BlockSpec((blocks, 1, span, tile), index)

    virt, occ, table, *packs = pl.pallas_call(
        rest_body,
        out_shape=[
            jax.ShapeDtypeStruct((2, half_rows, CAP * tile), jnp.bfloat16),
            jax.ShapeDtypeStruct((2, FROWS, SLABS * FROWS), jnp.bfloat16),
            jax.ShapeDtypeStruct((SLABS, VT), jnp.int32),
        ] + [jax.ShapeDtypeStruct((OCC, CAP * tile, LANES), jnp.bfloat16)] * count,
        grid_spec=pltpu.PrefetchScalarGridSpec(
            num_scalar_prefetch=2,
            grid=(CAP,),
            in_specs=[
                pl.BlockSpec((tile, OCC, cols), lambda q, mask, ids: (tile_of(mask, ids[0], q), 0, 0)),
                half_block(0),
                half_block(1),
                pl.BlockSpec(occ_density.shape, lambda q, mask, ids: (0, 0)),
            ],
            out_specs=[
                pl.BlockSpec((2, half_rows, tile), lambda q, mask, ids: (0, 0, q)),
                pl.BlockSpec((2, FROWS, SLABS * FROWS), lambda q, mask, ids: (0, 0, 0)),
                pl.BlockSpec(memory_space=pltpu.SMEM),
            ] + [pl.BlockSpec((OCC, tile, LANES), lambda q, mask, ids: (0, q, 0))] * count,
        ),
        compiler_params=pltpu.CompilerParams(vmem_limit_bytes=VMEM),
        cost_estimate=pl.CostEstimate(flops=3 << 30, bytes_accessed=12 << 20, transcendentals=0),
    )(mask, ids, three_index, by_half, by_half, occ_density)
    return packs, virt, occ, table


def density_body(slabs, shape_of, begins, ends, *refs):
    table_ref, ids_ref, *refs = refs
    count = len(slabs)
    sources = [[refs.pop(0) for _ in range(pieces)] for pieces in shape_of]
    virt_in, occ_in, *refs = refs
    if not begins:
        partial, *refs = refs
    out, packs, virt_ref, occ_ref, total, mixed, result, in_sems, out_sems = refs
    depth = sources[0][0].shape[1]
    half_rows = virt_ref.shape[1]
    blocks = half_rows // SPAN
    tile = depth // CAP
    arrivals = []
    for n, parts in enumerate(sources):
        step = OCC // len(parts)
        arrivals.append([
            pltpu.make_async_copy(
                ref, packs.at[n, pl.ds(m * step, step), pl.ds(0, depth), :], in_sems.at[2 * n + m]
            )
            for m, ref in enumerate(parts)
        ])
    arrivals.append([pltpu.make_async_copy(virt_in, virt_ref, in_sems.at[2 * count])])
    arrivals.append([pltpu.make_async_copy(occ_in, occ_ref, in_sems.at[2 * count + 1])])
    if not begins:
        arrivals.append([pltpu.make_async_copy(partial, total, in_sems.at[2 * count + 2])])
    for n in [0, count] + list(range(1, count)) + list(range(count + 1, len(arrivals))):
        for copy in arrivals[n]:
            copy.start()
    for n in range(count):
        packs[n, :, depth:depth + FINE, :] = jnp.zeros((OCC, FINE, LANES), jnp.bfloat16)
    perm = permutation(True) if ends else None
    waited = set()

    def arrived(n):
        if n not in waited:
            waited.add(n)
            for copy in arrivals[n]:
                copy.wait()

    arrived(count)
    if not begins:
        arrived(count + 2)
    for n, slab in enumerate(slabs):
        if slab >= 2:
            continue
        arrived(n)
        for i in range(0, OCC, 2):
            both = jnp.concatenate([packs[n, i, :depth], packs[n, i + 1, :depth]], axis=1)
            y = dot(virt_ref[slab], both)
            for j in range(2):
                part = y[:, j * LANES:(j + 1) * LANES]
                total[slab, i + j] = part if begins else part + total[slab, i + j]
    for n in range(len(arrivals)):
        arrived(n)
    fresh = [which for which in range(2) if begins and which not in slabs]
    departures = []
    for which in range(2):
        half = ids_ref[1] if which == 0 else 1 - ids_ref[1]
        weights = jnp.concatenate([occ_ref[which][:, s * FROWS:(s + 1) * FROWS] for s in slabs], axis=1)
        for first in range(0, half_rows, 2 * FINE):
            columns = []
            for row in (first, first + FINE):
                start = row // SPAN * (HALVES * SPAN) + row % SPAN + half * SPAN
                parts = []
                for n, s in enumerate(slabs):
                    base = table_ref[s, start // tile]
                    at = pl.multiple_of(jnp.where(base < 0, depth, base + start % tile), FINE)
                    parts.append(packs[n, :, pl.ds(at, FINE), :].reshape(FROWS, LANES))
                columns.append(jnp.concatenate(parts, axis=0))
            y = dot(weights, jnp.concatenate(columns, axis=1))
            for n in range(2):
                row = first + n * FINE
                part = y[:, n * LANES:(n + 1) * LANES].reshape(OCC, FINE, LANES)
                if which not in fresh:
                    part = part + total[which, :, row:row + FINE, :]
                if ends:
                    mixed[which, :, row:row + FINE, :] = part.astype(jnp.bfloat16)
                else:
                    total[which, :, row:row + FINE, :] = part
        if not ends:
            copy = pltpu.make_async_copy(total.at[which], out.at[which], out_sems.at[which])
            copy.start()
            departures.append(copy)
            continue
        for first in range(0, half_rows, 2 * GROUP):
            pair = transpose_rows(perm, [
                mixed[which, :, row:row + GROUP, :].reshape(ROWS, LANES) for row in (first, first + GROUP)
            ])
            for n in range(2):
                at = (first + n * GROUP) * OCC
                result[which, at:at + ROWS, :] = pair[n]
        for b in range(blocks):
            place = block_of(b * HALVES + half, ids_ref[0] % 2, HALVES * blocks)
            start = pl.multiple_of(place * SPAN * OCC, SPAN * OCC)
            copy = pltpu.make_async_copy(
                result.at[which, pl.ds(b * SPAN * OCC, SPAN * OCC), :],
                out.at[pl.ds(start, SPAN * OCC), :],
                out_sems.at[which * blocks + b],
            )
            copy.start()
            departures.append(copy)
    for copy in departures:
        copy.wait()


def density(table, ids, slabs, packs, virt, occ, partial=None, ends=True):
    packs = [pack if isinstance(pack, list) else [pack] for pack in packs]
    shape_of = [len(pack) for pack in packs]
    depth = packs[0][0].shape[1]
    half_rows = virt.shape[1]
    rows = 2 * half_rows * OCC
    sums = (2, OCC, half_rows, LANES)
    begins = partial is None
    share = len(slabs) * LANES
    extra = [] if begins else [partial]
    return pl.pallas_call(
        functools.partial(density_body, slabs, shape_of, begins, ends),
        out_shape=jax.ShapeDtypeStruct((rows, LANES), jnp.bfloat16) if ends else jax.ShapeDtypeStruct(sums, jnp.float32),
        grid_spec=pltpu.PrefetchScalarGridSpec(
            num_scalar_prefetch=2,
            grid=(1,),
            in_specs=[pl.BlockSpec(memory_space=pl.ANY)] * (sum(shape_of) + 2 + len(extra)),
            out_specs=pl.BlockSpec(memory_space=pl.ANY),
            scratch_shapes=[
                pltpu.VMEM((len(slabs), OCC, depth + FINE, LANES), jnp.bfloat16),
                pltpu.VMEM(virt.shape, jnp.bfloat16),
                pltpu.VMEM(occ.shape, jnp.bfloat16),
                pltpu.VMEM(sums, jnp.float32),
                pltpu.VMEM(sums if ends else (OCC, LANES), jnp.bfloat16),
                pltpu.VMEM((2, half_rows * OCC, LANES) if ends else (OCC, LANES), jnp.bfloat16),
                pltpu.SemaphoreType.DMA((2 * len(slabs) + 3,)),
                pltpu.SemaphoreType.DMA((2 * half_rows // SPAN,)),
            ],
        ),
        compiler_params=pltpu.CompilerParams(vmem_limit_bytes=24 << 20),
        cost_estimate=pl.CostEstimate(
            flops=1 if ends else share * (rows * depth // 2 + 2 * rows * ROWS),
            bytes_accessed=1 if ends else share * OCC * depth * 2 + rows * LANES * 2,
            transcendentals=0,
        ),
    )(table, ids, *(piece for pack in packs for piece in pack), virt, occ, *extra)


def assemble_body(*refs):
    count = len(refs) - 5
    ins, out = refs[:count], refs[count]
    arrived, whole, in_sems, out_sems = refs[count + 1:]
    rows = out.shape[0]
    peers = ins[0].shape[0] // rows
    cols = out.shape[2] // peers
    steps = peers // INNER

    core = lax.axis_index("occ") % 2

    def arrivals(n):
        part = pl.ds(pl.multiple_of(block_of(n, core, steps) * INNER * rows, INNER * rows), INNER * rows)
        return [
            pltpu.make_async_copy(ref.at[part], arrived.at[k, part], in_sems.at[n, k]) for k, ref in enumerate(ins)
        ]

    def departure(n):
        part = pl.ds(pl.multiple_of(n * INNER * cols, INNER * cols), INNER * cols)
        return pltpu.make_async_copy(whole.at[:, :, part], out.at[:, :, part], out_sems.at[n])

    def fetch(n, carry):
        for copy in arrivals(n):
            copy.start()
        return carry

    def place(n, carry):
        for copy in arrivals(n):
            copy.wait()
        for m in range(INNER):
            at = pl.multiple_of((block_of(n, core, steps) * INNER + m) * rows, rows)
            for k in range(count):
                first = pl.multiple_of((n * INNER + m) * cols + k * LANES, LANES)
                whole[:, :, pl.ds(first, LANES)] = arrived[k, pl.ds(at, rows)]
        departure(n).start()
        return carry

    def leave(n, carry):
        departure(n).wait()
        return carry

    lax.fori_loop(0, steps, fetch, 0)
    lax.fori_loop(0, steps, place, 0)
    lax.fori_loop(0, steps, leave, 0)


def assemble(parts, peers, cols):
    rows = parts[0].shape[0] // peers
    shape = (rows, OCC, peers * cols)
    return pl.pallas_call(
        assemble_body,
        out_shape=jax.ShapeDtypeStruct(shape, jnp.bfloat16),
        in_specs=[pl.BlockSpec(memory_space=pl.ANY)] * len(parts),
        out_specs=pl.BlockSpec(memory_space=pl.ANY),
        scratch_shapes=[
            pltpu.VMEM((len(parts),) + parts[0].shape, jnp.bfloat16),
            pltpu.VMEM(shape, jnp.bfloat16),
            pltpu.SemaphoreType.DMA((peers // INNER, len(parts))),
            pltpu.SemaphoreType.DMA((peers // INNER,)),
        ],
        compiler_params=pltpu.CompilerParams(vmem_limit_bytes=VMEM),
        cost_estimate=pl.CostEstimate(
            flops=0, bytes_accessed=4 * rows * OCC * shape[2], transcendentals=0
        ),
    )(*parts)


def place_body(part, _, out, sems):
    rows = out.shape[0]
    peers = part.shape[0] // rows
    cols = out.shape[2] // peers
    core = lax.axis_index("occ") % 2
    copies = []
    for m in range(peers):
        place = block_of(m // INNER, core, peers // INNER) * INNER + m % INNER
        copy = pltpu.make_async_copy(
            part.at[pl.ds(place * rows, rows)],
            out.at[:, :, pl.ds((m + 1) * cols - LANES, LANES)],
            sems.at[m],
        )
        copy.start()
        copies.append(copy)
    for copy in copies:
        copy.wait()


def place_last(part, whole):
    peers = part.shape[0] // whole.shape[0]
    return pl.pallas_call(
        place_body,
        out_shape=jax.ShapeDtypeStruct(whole.shape, whole.dtype),
        in_specs=[pl.BlockSpec(memory_space=pltpu.VMEM), pl.BlockSpec(memory_space=pl.ANY)],
        out_specs=pl.BlockSpec(memory_space=pl.ANY),
        scratch_shapes=[pltpu.SemaphoreType.DMA((peers,))],
        input_output_aliases={1: 0},
        compiler_params=pltpu.CompilerParams(vmem_limit_bytes=8 << 20),
        cost_estimate=pl.CostEstimate(flops=0, bytes_accessed=4 * part.size, transcendentals=0),
    )(part, whole)


def exchange_groups(peers):
    groups = []
    for parity in range(2):
        for core in range(2):
            groups.append([
                (2 * (((k // INNER) % HALVES) ^ parity) + core) * peers + k
                for k in (block_of(m // INNER, core, peers // INNER) * INNER + m % INNER for m in range(peers))
            ])
    return groups


def local(three_index, tile_mask, occ_density, virt_density):
    virt_count = three_index.shape[0]
    peers = lax.axis_size("aux")
    own = lax.axis_index("occ")
    my_half = (lax.axis_index("aux") // INNER) % HALVES
    by_half = virt_density.reshape(peers // (HALVES * INNER), HALVES, -1, virt_count)

    head = first_pack(tile_mask, three_index)
    ids = jnp.stack(lax.optimization_barrier((own, my_half, head))[:2]).astype(jnp.int32)
    others, *weights = rest_pack(tile_mask, ids, three_index, by_half, occ_density)
    virt, occ, table = (pltpu.with_memory_space_constraint(array, pltpu.HBM) for array in weights)
    mine = [head] + others

    chip_pairs = [(s, s ^ 2) for s in range(SLABS)]
    core_pairs = [(s, s ^ 1) for s in range(SLABS)]
    groups = exchange_groups(peers)
    done = []
    arrivals = [lax.ppermute(part, "occ", chip_pairs) for part in mine]
    last = len(mine) - 1
    besides = [lax.ppermute(part, "occ", core_pairs) for part in mine]
    for k, part in enumerate(mine):
        across = arrivals[k]
        beside = besides[k]
        partial = None
        if k in (0, last):
            own_part = part if k == 0 else lax.optimization_barrier((part, gamma))[0]
            partial = density(table, ids, (0, 2), (own_part, beside), virt, occ, ends=False)
        before = (mine[1], partial) if k == 0 else (gamma, partial) if k == last else (gamma,)
        across, *before = lax.optimization_barrier((across,) + before)
        diagonal = [lax.ppermute(half, "occ", core_pairs) for half in jnp.split(across, 2, axis=0)]
        if partial is None:
            gamma = density(table, ids, (0, 1, 2, 3), (part, across, beside, diagonal), virt, occ)
        else:
            gamma = density(table, ids, (1, 3), (across, diagonal), virt, occ, partial=before[1])
        done.append(lax.all_to_all(
            gamma.reshape(virt_count, OCC, -1), ("occ", "aux"),
            split_axis=0, concat_axis=0, axis_index_groups=groups, tiled=True,
        ))
    return place_last(done[-1], assemble(done[:-1], peers, three_index.shape[2]))


def solution(mesh):
    return jax.shard_map(
        local,
        mesh=mesh,
        in_specs=(P(None, "occ", "aux"), P(), P(), P()),
        out_specs=P("aux", "occ", None),
        check_vma=False,
    )
```
